512 devices in a mesh: grp: 16 (over y, core), basin: 32 (over z, x).
Axes of the slice: x: 4, y: 8, z: 8, core: 2. Of those that a mesh axis runs over, the one named last changes fastest.
Arguments:
- leaf_features: bfloat16 [16, 128, 65536], P(None, None, ('grp', 'basin')), may hold values from -6 to 6
- node_features: bfloat16 [16, 128, 5632], P(None, None, ('grp', 'basin')), may hold values from -6 to 6
- w_in: bfloat16 [512, 128], replicated, may hold values from -0.5 to 0.5
- w_out: bfloat16 [7, 512], replicated, may hold values from -0.5 to 0.5
- leaf_var: float32 [65536], P(('grp', 'basin')), may hold values from 0.5 to 18, as said below
- node_var: float32 [5120], P(('grp', 'basin')), may hold values from 0.5 to 2
- inner_var: float32 [511], replicated, may hold values from 0.5 to 2
- sub_sizes: int32 [512, 9], P(('grp', 'basin')), may hold values from 1 to 32, 128 in all within a row
Outputs:
- reconciled: float32 [112, 65536], P(None, ('grp', 'basin'))
- residual: float32 [112, 65536], P(None, ('grp', 'basin'))
The draws below stay inside these ranges and needn't reach their ends.
Inputs may be any that keep to these rules, and one draw needn't show every extreme that they name: `sub_sizes`: each device's row sums to 128, and its largest entry is exactly 32. `leaf_var`: positive variances.
All inputs are finite; a program needn't handle non-finite values.
Results may differ from the reference program's by a relative error of at most 0.0026.
Values sent between devices are 32-bit elements; how exact they have to be, the bound alone decides.
A program may use at most 64 MiB of HBM per device.

```python
import math
from functools import partial
import jax
import jax.numpy as jnp
import numpy as np
from jax import lax

H = 512
F = 128
DAYS = 7
MEMBERS = 16
LEAF_DEV = 128
SUB_DEV = 9
ITERS = 3
COLS = 112
LEAVES = 65536
N_GRP = 16
N_BASIN = 32
DEVICES = 512


def draw_leaf_var(key, part):
    device_key, leaf_key = jax.random.split(key)
    device_count = LEAVES // LEAF_DEV
    device_scale = jnp.exp(jax.random.uniform(device_key, (device_count, 1), jnp.float32, 0.0, math.log(9.0)))
    leaf_scale = jnp.exp(jax.random.uniform(leaf_key, (device_count, LEAF_DEV), jnp.float32, math.log(0.5), math.log(2.0)))
    return (device_scale * leaf_scale).reshape(LEAVES)


def shard_levels(own_key, dims, pieces, low, top_value):
    def one(dim, shards_of):
        draws = jax.random.uniform(jax.random.fold_in(jax.random.fold_in(own_key, 6), dim), (shards_of,), jnp.float32, low / len(pieces), top_value / len(pieces))
        return jnp.repeat(jnp.exp(draws), dims[dim] // shards_of).reshape((-1,) + (1,) * (len(dims) - dim - 1))

    factor_of = one(*pieces[0])
    for cut in pieces[1:]:
        factor_of = factor_of * one(*cut)
    return factor_of


def profile(count, total, bound, skew):
    weights = [(1 << 20) // math.isqrt(grade ** skew) + 1 for grade in range(2, count + 1)]
    surplus, given = total - bound - (count - 1), [1] * (count - 1)
    while surplus > 0:
        free = [i for i in range(count - 1) if given[i] < bound]
        whole, left = sum([weights[i] for i in free]), surplus
        for i in free:
            addition = min(bound - given[i], max(1, left * weights[i] // whole), surplus)
            given[i] = given[i] + addition
            surplus = surplus - addition
    return np.array([bound] + given)


def uneven(key, amount, total, most, slope):
    if amount == 2:
        one = jax.random.randint(key, (), max(1, total - most), min(most, total - 1) + 1)
        return jnp.stack([one, total - one])
    tallies = jnp.asarray(profile(amount, total, most, slope), jnp.int32)
    pairs = (amount - 1) // 2
    source_of, taker = tallies[1:1 + 2 * pairs:2], tallies[2:2 + 2 * pairs:2]
    slack = jnp.minimum(source_of - 1, most - taker)
    shifted = jax.random.randint(jax.random.fold_in(key, 1), (pairs,), 0, 1 << 20) % (slack + 1)
    tallies = tallies.at[1:1 + 2 * pairs:2].set(source_of - shifted).at[2:2 + 2 * pairs:2].set(taker + shifted)
    return tallies[jax.random.permutation(jax.random.fold_in(key, 2), amount)]


def bell_draw(own_key, shape, scale, most, shards=(), kind=jnp.bfloat16):
    factor_of = shard_levels(own_key, shape, shards, -0.22, 0.18) if shards else 1.0
    array = jax.random.normal(own_key, shape, jnp.float32) * scale * factor_of
    return jnp.minimum(jnp.maximum(array, -most), most).astype(kind)


def setup_inputs(seed: int = 0) -> dict:
    streams_of = jax.random.split(jax.random.key(seed), 9)
    leaf_features = bell_draw(streams_of[0], (MEMBERS, F, LEAVES), 1.0, 6.0, ((2, 512),))
    node_features = bell_draw(streams_of[1], (MEMBERS, F, (SUB_DEV + 2) * DEVICES), 1.0, 6.0, ((2, 512),))
    w_in = bell_draw(streams_of[2], (H, F), F ** -0.5, 0.5)
    w_out = bell_draw(streams_of[3], (DAYS, H), (H // 4) ** -0.5, 0.5)
    leaf_var = draw_leaf_var(jax.random.fold_in(streams_of[8], 71), 0)
    node_var = jnp.clip(jnp.exp(math.log(2.0) - 1.3862944 * jax.random.uniform(streams_of[5], ((SUB_DEV + 1) * DEVICES,), jnp.float32) ** shard_levels(streams_of[5], ((SUB_DEV + 1) * DEVICES,), ((0, 512),), -0.2, 0.2)), 0.5, 2.0)
    inner_var = jnp.clip(jnp.exp(jax.random.uniform(streams_of[6], (DEVICES - 1,), jnp.float32, math.log(0.5), math.log(2.0))), 0.5, 2.0)
    sub_sizes = jax.vmap(lambda own: uneven(own, SUB_DEV, LEAF_DEV, LEAF_DEV // 4, 2))(jax.random.split(streams_of[7], DEVICES)).reshape((DEVICES, SUB_DEV)).astype(jnp.int32)
    return {"leaf_features": leaf_features, "node_features": node_features, "w_in": w_in, "w_out": w_out, "leaf_var": leaf_var, "node_var": node_var, "inner_var": inner_var, "sub_sizes": sub_sizes}


exact = lax.Precision.HIGHEST


def member_block(w_in, w_out, features):
    hidden = jnp.einsum("hf,mfn->mhn", w_in.astype(jnp.float32), features.astype(jnp.float32), precision=exact)
    hidden = lax.optimization_barrier(jax.nn.silu(hidden).astype(jnp.bfloat16))
    return jnp.einsum("dh,mhn->mdn", w_out.astype(jnp.float32), hidden.astype(jnp.float32), precision=exact)


def membership(sizes):
    ends = jnp.cumsum(sizes)
    starts = ends - sizes
    position = jnp.arange(LEAF_DEV, dtype=jnp.int32)[:, None]
    return ((position >= starts[None, :]) & (position < ends[None, :])).astype(jnp.float32)


def reference(leaf_features, node_features, w_in, w_out, leaf_var, node_var, inner_var, sub_sizes):
    device_count = N_GRP * N_BASIN
    upper = SUB_DEV + 2
    mapper = partial(member_block, w_in, w_out)
    leaf_blocks = leaf_features.reshape(MEMBERS, F, device_count, LEAF_DEV).transpose(2, 0, 1, 3)
    soft_leaf = jax.nn.softplus(lax.map(mapper, leaf_blocks)).reshape(device_count, COLS, LEAF_DEV)
    upper_blocks = node_features.reshape(MEMBERS, F, device_count, upper).transpose(2, 0, 1, 3)
    soft_upper = jax.nn.softplus(lax.map(mapper, upper_blocks)).reshape(device_count, COLS, upper)
    table = jax.vmap(membership)(sub_sizes)
    node_scale = node_var.reshape(device_count, SUB_DEV + 1)
    sub_scale = 1.0 / (sub_sizes.astype(jnp.float32) * node_scale[:, :SUB_DEV])
    sub_terms = soft_upper[:, :, :SUB_DEV] / node_scale[:, None, :SUB_DEV]
    device_terms = soft_upper[:, :, SUB_DEV] / node_scale[:, SUB_DEV:SUB_DEV + 1]
    owners = jnp.arange(device_count, dtype=jnp.int32)
    own_var = inner_var[jnp.maximum(owners - 1, 0)]
    own_terms = jnp.where((owners >= 1)[:, None], soft_upper[:, :, SUB_DEV + 1] / own_var[:, None], 0.0)
    levels = device_count.bit_length() - 1
    inner_rhs = jnp.zeros((device_count, COLS), jnp.float32)
    weights_up = []
    for height in range(1, levels + 1):
        span = 2 ** height
        node_owner = jnp.arange(device_count // span, dtype=jnp.int32) * span + span // 2
        inner_rhs = inner_rhs + jnp.repeat(own_terms[node_owner], span, axis=0)
        weights_up.append(1.0 / (LEAF_DEV * span * inner_var[node_owner - 1]))
    leaf_scale = leaf_var.reshape(device_count, LEAF_DEV)
    rhs = soft_leaf / leaf_scale[:, None, :]
    rhs = rhs + jnp.einsum("dcs,dls->dcl", sub_terms, table, precision=exact)
    rhs = rhs + (device_terms + inner_rhs)[:, :, None]

    def operate(field):
        sub_sums = jnp.einsum("dcl,dls->dcs", field, table, precision=exact)
        back = jnp.einsum("dcs,dls->dcl", sub_sums * sub_scale[:, None, :], table, precision=exact)
        device_total = jnp.sum(field, axis=2)
        inner = jnp.zeros((device_count, COLS), jnp.float32)
        for height in range(1, levels + 1):
            span = 2 ** height
            node_sums = jnp.sum(device_total.reshape(device_count // span, span, COLS), axis=1)
            inner = inner + jnp.repeat(node_sums * weights_up[height - 1][:, None], span, axis=0)
        device_part = device_total / (LEAF_DEV * node_scale[:, SUB_DEV:SUB_DEV + 1])
        return field / leaf_scale[:, None, :] + back + (device_part + inner)[:, :, None]

    solution = jnp.zeros_like(rhs)
    residual = rhs
    direction = rhs
    norm_now = jnp.sum(residual * residual, axis=(0, 2))
    for iteration in range(ITERS):
        applied = operate(direction)
        step_size = norm_now / jnp.sum(direction * applied, axis=(0, 2))
        solution = solution + step_size[None, :, None] * direction
        residual = residual - step_size[None, :, None] * applied
        norm_next = jnp.sum(residual * residual, axis=(0, 2))
        direction = residual + (norm_next / norm_now)[None, :, None] * direction
        norm_now = norm_next
    reconciled = solution.transpose(1, 0, 2).reshape(COLS, LEAVES)
    return reconciled, residual.transpose(1, 0, 2).reshape(COLS, LEAVES)
```

```python
import jax
import jax.numpy as jnp
from jax import lax
from jax.experimental import pallas as pl
from jax.experimental.pallas import tpu as pltpu
from jax.sharding import PartitionSpec as P

MESH = pl.DeviceIdType.MESH
F32 = jnp.float32
BF16 = jnp.bfloat16
LEAF = 128
GRP = 16
BASIN = 32
PLACE = (0, 1, 2, 3, 4, 5, 6, 8, 9, 10, 7)
INNER = 7


def iota(shape, axis):
    return lax.broadcasted_iota(jnp.int32, shape, axis)


def exact_dot(a, b):
    return jnp.dot(a, b, precision=lax.Precision.HIGHEST, preferred_element_type=F32)


def exact_dot_t(a, b):
    return lax.dot_general(
        a, b, (((1,), (1,)), ((), ())), precision=lax.Precision.HIGHEST, preferred_element_type=F32
    )


def softplus(z):
    return jnp.maximum(z, 0.0) + jnp.log1p(jnp.exp(-jnp.abs(z)))


def pick(condition, value=1.0):
    return jnp.where(condition, value, 0.0).astype(F32)


def owner_of(index, height):
    return ((index >> height) << height) + (1 << (height - 1))


def xor_lanes(x, slot, bit):
    step = 8 * bit
    if step == 64:
        return pltpu.roll(x, 64, 1)
    return jnp.where((slot & bit) != 0, pltpu.roll(x, step, 1), pltpu.roll(x, 128 - step, 1))


def xor_rows(x, bit):
    if bit >= 8:
        far = bit // 8
        return jnp.concatenate([x[i ^ far : (i ^ far) + 1] for i in range(4)], axis=0)
    if bit == 4:
        return pltpu.roll(x, 4, 1)
    odd = (iota((4, 8, 128), 1) & bit) != 0
    return jnp.where(odd, pltpu.roll(x, bit, 1), pltpu.roll(x, 8 - bit, 1))


def total(x):
    y = (x[0] + x[1]) + (x[2] + x[3])
    for step in (4, 2, 1):
        y = y + pltpu.roll(y, step, 0)
    for step in (64, 32, 16, 8):
        y = y + pltpu.roll(y, step, 1)
    return y


def kernel(
    lf, nf, w_in, w_out, leaf_var, node_var, inner_var, sub_sizes,
    x_out, r_out,
    z_buf, up_buf, v_buf, n_buf, w_low, w_top, send1, recv1, send2, recv2, send3, recv3, rows_buf,
    ss1, rs1, ss2, rs2, ss3, rs3,
):
    g = lax.axis_index("grp")
    b = lax.axis_index("basin")
    q = g * BASIN + b
    barrier = pltpu.get_barrier_semaphore()
    for step in range(1, GRP):
        pl.semaphore_signal(barrier, inc=1, device_id=(lax.rem(g + step, GRP), b), device_id_type=MESH)
    for step in range(1, BASIN):
        pl.semaphore_signal(barrier, inc=1, device_id=(g, lax.rem(b + step, BASIN)), device_id_type=MESH)

    half = w_in[...] * jnp.asarray(0.5, BF16)
    w2 = w_out[...]

    def network(features):
        h = jnp.dot(half, features, preferred_element_type=F32)
        hidden = (h + h * jnp.tanh(h)).astype(BF16)
        return jnp.dot(w2, hidden, preferred_element_type=F32)

    z_buf[...] = jnp.zeros_like(z_buf)
    for pair in range(8):
        z = network(jnp.concatenate([lf[2 * pair], lf[2 * pair + 1]], axis=1))
        z_buf[2 * pair, :7, :] = z[:, :128]
        z_buf[2 * pair + 1, :7, :] = z[:, 128:]
    lane11 = iota((11, 128), 1)
    node11 = iota((11, 128), 0)
    lane_of = jnp.where(node11 < 7, node11, jnp.where(node11 == 10, INNER, node11 + 1))
    placed = []
    for part in range(2):
        both = jnp.zeros((128, 128), F32)
        for j in range(8):
            at = pick(lane11 == lane_of + 16 * j).astype(BF16)
            both = both + jnp.dot(nf[8 * part + j], at, preferred_element_type=F32)
        placed.append(both.astype(BF16))
    zn = network(jnp.concatenate(placed, axis=1))
    soft_up = softplus(zn)
    up_buf[...] = jnp.zeros_like(up_buf)
    for m in range(16):
        part = soft_up[:, 128 * (m // 8) : 128 * (m // 8) + 128]
        shift = 16 * (m % 8)
        moved = part if shift == 0 else jnp.concatenate([part[:, shift:], part[:, :shift]], axis=1)
        up_buf[m, :7, :] = moved

    leaf_row = iota((1, 128), 1)
    leaf_i = iota((128, 128), 0)
    leaf_j = iota((128, 128), 1)
    label_row = jnp.zeros((1, 128), jnp.int32)
    label_i = jnp.zeros((128, 128), jnp.int32)
    end = jnp.int32(0)
    for s in range(9):
        end = end + sub_sizes[0, s]
        label_row = label_row + (leaf_row >= end).astype(jnp.int32)
        label_i = label_i + (leaf_i >= end).astype(jnp.int32)
    scale_row = jnp.zeros((1, 128), F32)
    lane16 = iota((1, 128), 1)
    inv_row = jnp.zeros((1, 128), F32)
    one_row = jnp.ones((1, 128), F32)
    for s in range(9):
        var = node_var[0, s] * one_row
        scale_row = jnp.where(label_row == s, 1.0 / (sub_sizes[0, s].astype(F32) * var), scale_row)
        inv_row = jnp.where(lane16 == PLACE[s], 1.0 / var, inv_row)
    dev_var = node_var[0, 9] * one_row
    inv_row = jnp.where(lane16 == PLACE[9], 1.0 / dev_var, inv_row)
    leaf_inv = 1.0 / leaf_var[...]
    op1 = (
        jnp.where(label_i == label_row, scale_row, 0.0)
        + 1.0 / (LEAF * dev_var)
        + jnp.where(leaf_i == leaf_j, leaf_inv, 0.0)
    )
    op2 = exact_dot(op1, op1)
    op3 = exact_dot(op2, op1)
    n1 = jnp.sum(op1, axis=0, keepdims=True)
    n2 = jnp.sum(op2, axis=0, keepdims=True)
    n3 = jnp.sum(op3, axis=0, keepdims=True)
    row8 = iota((8, 128), 0)
    low = jnp.where(row8 == 0, one_row, jnp.where(row8 == 1, n1, jnp.where(row8 == 2, n2, 0.0)))
    high = exact_dot(low, op3)
    n4 = high[1:2]
    n5 = high[2:3]
    powers = (one_row, n1, n2, n3, n4, n5)
    to_m = jnp.zeros((8, 128), F32)
    to_n = jnp.zeros((8, 128), F32)
    for k in range(6):
        to_m = jnp.where(row8 == k, powers[k], to_m)
        if k:
            to_n = jnp.where(row8 == k - 1, powers[k], to_n)
    n_buf[...] = to_m
    n_col = jnp.sum(to_n, axis=1, keepdims=True)

    soft_leaf = softplus(z_buf[...].reshape(128, 128))
    up = up_buf[...].reshape(128, 128)
    node16 = iota((16, 128), 0)
    table = jnp.zeros((16, 128), F32)
    for s in range(9):
        table = jnp.where((node16 == PLACE[s]) & (label_row == s), 1.0, table)
    table = jnp.where(node16 == PLACE[9], 1.0, table)
    scaled = (up * inv_row)[:, :16]
    b0 = soft_leaf * leaf_inv + exact_dot(scaled, table)
    v1 = exact_dot(b0, op1)
    v2 = exact_dot(b0, op2)
    v3 = exact_dot(b0, op3)
    v_buf[0] = b0
    v_buf[1] = v1
    v_buf[2] = v2
    v_buf[3] = v3

    lanes = iota((128, 128), 1)
    pack = exact_dot_t(b0, jnp.concatenate([to_m, jnp.zeros((120, 128), F32)], axis=0))
    products = (b0 * b0, b0 * v1, v1 * v1, v1 * v2, v2 * v2, v2 * v3)
    for k in range(6):
        pack = jnp.where(lanes == 8 + k, jnp.sum(products[k], axis=1, keepdims=True), pack)
    inner_row = inner_var[...]
    inner_at = iota((1, 511), 1)
    own_var = jnp.sum(jnp.where(inner_at == jnp.maximum(q - 1, 0), inner_row, 0.0), axis=1, keepdims=True)
    own_gain = jnp.where(q >= 1, 1.0 / own_var, 0.0)
    pack = jnp.where(lanes == INNER, up * own_gain, pack)
    pack = pack.reshape(16, 8, 128)
    lanes3 = iota((16, 8, 128), 2)
    pack = jnp.where(lanes3 == 6, n_col[None], pack)
    send1[...] = pack

    pl.semaphore_wait(barrier, GRP + BASIN - 2)

    for step in range(1, GRP):
        to = lax.rem(g + step, GRP)
        pltpu.make_async_remote_copy(
            src_ref=send1.at[to], dst_ref=recv1.at[g], send_sem=ss1, recv_sem=rs1,
            device_id=(to, b), device_id_type=MESH,
        ).start()
    recv1[pl.ds(g, 1)] = send1[pl.ds(g, 1)]

    at = iota((32, 511), 1) + 1
    spread = jnp.where((at & 31) == iota((32, 511), 0), inner_row, 0.0)
    at_col = iota((511, 128), 0) + 1
    to_slot = pick((at_col >> 5) == (iota((511, 128), 1) >> 3))
    var_of = exact_dot(spread, to_slot)
    low_row = iota((32, 32), 0)
    low_col = iota((32, 32), 1)
    row32 = iota((32, 128), 0)
    lane32 = iota((32, 128), 1)
    inverse = jnp.where((row32 == 0) & (lane32 < 8), 0.0, 1.0 / jnp.where((row32 == 0) & (lane32 < 8), 1.0, var_of))
    low_all = jnp.zeros((32, 32), F32)
    for h in range(1, 6):
        chosen = pick(low_col == owner_of(low_row, h))
        low_all = low_all + chosen
        w_low[h - 1] = exact_dot(chosen, inverse) * (1.0 / (LEAF * 2**h))
    from_lane = iota((128, 128), 0)
    top_all = jnp.zeros((128, 128), F32)
    same_day = (from_lane & 7) == (lanes & 7)
    for h in range(1, 5):
        chosen = pick(same_day & ((from_lane >> 3) == owner_of(lanes >> 3, h)))
        top_all = top_all + chosen
        w_top[h - 1] = exact_dot(jnp.broadcast_to(inverse[0:1], (8, 128)), chosen) * (1.0 / (LEAF * 2 ** (h + 5)))
    lane8 = iota((8, 128), 1)
    pad8 = (lane8 & 7) == 7
    to_pad = pick(((lanes & 7) == 7) & ((from_lane & 7) == (lanes >> 3)) & ((lanes >> 3) < 7))
    from_pad = pick(((from_lane & 7) == 7) & ((lanes & 7) == (from_lane >> 3)) & ((from_lane >> 3) < 7))
    same_slot = (from_lane >> 3) == (lanes >> 3)
    to_n_lanes = jnp.concatenate([pick(same_slot & ((from_lane & 7) == k)) for k in range(5)], axis=1)

    pltpu.make_async_copy(recv1.at[pl.ds(0, GRP - 1)], recv1.at[pl.ds(0, GRP - 1)], rs1).wait()
    turned = recv1[...].reshape(128, 128).T
    sums = exact_dot(turned[8:16], to_pad)
    send2[...] = jnp.where(pad8, sums, turned[:8])

    for step in range(1, BASIN):
        to = lax.rem(b + step, BASIN)
        pltpu.make_async_remote_copy(
            src_ref=send2, dst_ref=recv2.at[b], send_sem=ss2, recv_sem=rs2,
            device_id=(g, to), device_id_type=MESH,
        ).start()
    recv2[pl.ds(b, 1)] = send2[...][None]
    pltpu.make_async_copy(recv2.at[pl.ds(0, BASIN - 1)], recv2.at[pl.ds(0, BASIN - 1)], rs2).wait()

    everything = recv2[...]
    fluct = exact_dot(jnp.sum(everything, axis=0), from_pad)
    p = [jnp.broadcast_to(fluct[k : k + 1], (8, 128)) for k in range(6)]
    own = recv2[:, INNER, :]
    m = [recv2[:, k, :].reshape(4, 8, 128) for k in range(6)]
    n_all = exact_dot(recv2[:, 6, :], to_n_lanes)
    n = [F32(LEAF)] + [n_all[:, 128 * k : 128 * k + 128].reshape(4, 8, 128) for k in range(5)]
    rho = exact_dot(low_all, own) + exact_dot(jnp.broadcast_to(own[0:1], (8, 128)), top_all)[0:1]
    rho = rho.reshape(4, 8, 128)
    slot8 = lane8 >> 3

    def inner(s):
        y = s
        u = jnp.zeros_like(s)
        for h in range(5):
            y = y + xor_rows(y, 1 << h)
            u = u + w_low[h].reshape(4, 8, 128) * y
        t = y[0]
        top = jnp.zeros((8, 128), F32)
        for h in range(4):
            t = t + xor_lanes(t, slot8, 1 << h)
            top = top + w_top[h] * t
        return u + top[None]

    def combine(c, e, shift):
        out = 0.0
        for j in range(len(c)):
            out = out + c[j] * m[j + shift] + e[j] * n[j + shift]
        return out

    def form(c, e, shift):
        whole = 0.0
        each = 0.0
        for j in range(len(c)):
            for k in range(j, len(c)):
                twice = 1.0 if j == k else 2.0
                t = j + k + shift
                whole = whole + (twice * c[j] * c[k]) * p[t]
                cross = c[j] * e[k] if j == k else c[j] * e[k] + c[k] * e[j]
                each = each + 2.0 * cross * m[t] + (twice * e[j]) * e[k] * n[t]
        return whole, each

    one = jnp.ones((8, 128), F32)
    d_c = [one]
    d_e = [rho]
    r_c = [one]
    r_e = [rho]
    whole, each = form(d_c, d_e, 0)
    norm = whole + total(each)
    rows_buf[0] = rho.reshape(32, 128)
    steps = []
    betas = []
    for it in range(3):
        s = combine(d_c, d_e, 0)
        image = inner(s)
        rows_buf[it + 1] = image.reshape(32, 128)
        whole, each = form(d_c, d_e, 1)
        curvature = whole + total(each + s * image)
        alpha = norm / curvature
        steps.append(alpha)
        if it == 2:
            break
        whole, each = form(d_c, d_e, 2)
        square = whole + total(each + image * (2.0 * combine(d_c, d_e, 1) + LEAF * image))
        after = alpha * alpha * square - norm
        beta = after / norm
        betas.append(beta)
        r_c = [a - alpha * i for a, i in zip(r_c + [0.0], [0.0] + d_c)]
        r_e = [a - alpha * i for a, i in zip(r_e + [0.0], [image] + d_e)]
        d_c = [a + beta * i for a, i in zip(r_c, d_c + [0.0])]
        d_e = [a + beta * i for a, i in zip(r_e, d_e + [0.0])]
        norm = after

    mine = [rows_buf[k, pl.ds(b, 1), :] for k in range(4)]
    d_c = [one[0:1]]
    d_e = [mine[0]]
    r_c = [one[0:1]]
    r_e = [mine[0]]
    x_c = [0.0] * 3
    x_e = [0.0] * 3
    for it in range(3):
        alpha = steps[it][0:1]
        for k in range(it + 1):
            x_c[k] = x_c[k] + alpha * d_c[k]
            x_e[k] = x_e[k] + alpha * d_e[k]
        r_c = [a - alpha * i for a, i in zip(r_c + [0.0], [0.0] + d_c)]
        r_e = [a - alpha * i for a, i in zip(r_e + [0.0], [mine[it + 1]] + d_e)]
        if it < 2:
            beta = betas[it][0:1]
            d_c = [a + beta * i for a, i in zip(r_c, d_c + [0.0])]
            d_e = [a + beta * i for a, i in zip(r_e, d_e + [0.0])]
    back = jnp.concatenate(r_e + x_e + [one[0:1]] + r_c[1:] + x_c + [jnp.zeros((114, 128), F32)], axis=0)
    send3[...] = back.T.reshape(16, 8, 128)

    for step in range(1, GRP):
        to = lax.rem(g + step, GRP)
        pltpu.make_async_remote_copy(
            src_ref=send3.at[to], dst_ref=recv3.at[g], send_sem=ss3, recv_sem=rs3,
            device_id=(to, b), device_id_type=MESH,
        ).start()
    recv3[pl.ds(g, 1)] = send3[pl.ds(g, 1)]
    rows = n_buf[...]
    zero_rows = jnp.zeros((8, 128), F32)
    row16 = iota((16, 128), 0)
    lift_r = jnp.zeros((16, 128), F32)
    lift_x = jnp.zeros((16, 128), F32)
    for k in range(4):
        lift_r = jnp.where(row16 == k, rows[k : k + 1], lift_r)
        if k < 3:
            lift_x = jnp.where(row16 == 4 + k, rows[k : k + 1], lift_x)
    pltpu.make_async_copy(recv3.at[pl.ds(0, GRP - 1)], recv3.at[pl.ds(0, GRP - 1)], rs3).wait()
    gains = recv3[...].reshape(128, 128)
    gains = jnp.where((leaf_i & 7) == 7, 0.0, gains)
    small = gains[:, :16]
    r = exact_dot(small, lift_r) + v_buf[0]
    x = exact_dot(small, lift_x)
    for k in range(3):
        r = r + gains[:, 8 + k : 9 + k] * v_buf[k + 1]
        x = x + gains[:, 11 + k : 12 + k] * v_buf[k]
    x_out[...] = x.reshape(16, 8, 128)
    r_out[...] = r.reshape(16, 8, 128)

    pltpu.make_async_copy(recv1.at[pl.ds(0, GRP - 1)], recv1.at[pl.ds(0, GRP - 1)], ss1).wait()
    pltpu.make_async_copy(recv2.at[pl.ds(0, BASIN - 1)], recv2.at[pl.ds(0, BASIN - 1)], ss2).wait()
    pltpu.make_async_copy(recv3.at[pl.ds(0, GRP - 1)], recv3.at[pl.ds(0, GRP - 1)], ss3).wait()


def on_device(leaf_features, node_features, w_in, w_out, leaf_var, node_var, inner_var, sub_sizes):
    vmem = pl.BlockSpec(memory_space=pltpu.VMEM)
    smem = pl.BlockSpec(memory_space=pltpu.SMEM)
    tile = jax.ShapeDtypeStruct((16, 8, 128), F32)
    x, r = pl.pallas_call(
        kernel,
        out_shape=(tile, tile),
        in_specs=[vmem, vmem, vmem, vmem, vmem, smem, vmem, smem],
        out_specs=(vmem, vmem),
        scratch_shapes=[
            pltpu.VMEM((16, 8, 128), F32),
            pltpu.VMEM((16, 8, 128), F32),
            pltpu.VMEM((4, 128, 128), F32),
            pltpu.VMEM((8, 128), F32),
            pltpu.VMEM((5, 32, 128), F32),
            pltpu.VMEM((4, 8, 128), F32),
            pltpu.VMEM((16, 8, 128), F32),
            pltpu.VMEM((16, 8, 128), F32),
            pltpu.VMEM((8, 128), F32),
            pltpu.VMEM((32, 8, 128), F32),
            pltpu.VMEM((16, 8, 128), F32),
            pltpu.VMEM((16, 8, 128), F32),
            pltpu.VMEM((4, 32, 128), F32),
        ]
        + [pltpu.SemaphoreType.DMA] * 6,
        compiler_params=pltpu.CompilerParams(
            collective_id=0, has_side_effects=True, vmem_limit_bytes=48 * 1024 * 1024
        ),
    )(
        leaf_features, node_features, w_in, w_out,
        leaf_var.reshape(1, -1), node_var.reshape(1, -1), inner_var.reshape(1, -1), sub_sizes,
    )
    return x[:, :7].reshape(112, 128), r[:, :7].reshape(112, 128)


def solution(mesh):
    return jax.shard_map(
        on_device,
        mesh=mesh,
        in_specs=(
            P(None, None, ("grp", "basin")),
            P(None, None, ("grp", "basin")),
            P(),
            P(),
            P(("grp", "basin")),
            P(("grp", "basin")),
            P(),
            P(("grp", "basin"), None),
        ),
        out_specs=(P(None, ("grp", "basin")), P(None, ("grp", "basin"))),
        check_vma=False,
    )
```

```python
import jax
import jax.numpy as jnp
from jax import lax
from jax.experimental import pallas as pl
from jax.experimental.pallas import tpu as pltpu
from jax.sharding import PartitionSpec as P

MESH = pl.DeviceIdType.MESH
F32 = jnp.float32
BF16 = jnp.bfloat16
LEAF = 128
GRP = 16
BASIN = 32
INNER = 7
CHUNKS = 4


def iota(shape, axis):
    return lax.broadcasted_iota(jnp.int32, shape, axis)


def far_first(sizes):
    a, b = sizes
    offsets = [(i, j) for i in range(a) for j in range(b) if i or j]
    return sorted(offsets, key=lambda o: -(min(o[0], a - o[0]) + min(o[1], b - o[1])))


def peer(index, offset, sizes):
    a, b = sizes
    return lax.rem(index // b + offset[0], a) * b + lax.rem(lax.rem(index, b) + offset[1], b)


def turn_out(x):
    y = pltpu.roll(x, 0, 1, stride=8, stride_axis=0)
    slot = iota((16, 128), 1) >> 3
    for k in (1, 2, 4, 8):
        y = jnp.where((slot & k) != 0, pltpu.roll(y, 16 - k, 0), y)
    return y


def turn_in(x, me):
    y = pltpu.roll(x, 0, 1, stride=8, stride_axis=0)
    away = (iota((16, 128), 1) >> 3) - me
    for k in (1, 2, 4, 8):
        y = jnp.where((away & k) != 0, pltpu.roll(y, 16 - k, 0), y)
    y = pltpu.roll(y, 0, 1, stride=8, stride_axis=0)
    return pltpu.roll(y, lax.rem(128 - 8 * me, 128), 1)


def exact_dot(a, b):
    return jnp.dot(a, b, precision=lax.Precision.HIGHEST, preferred_element_type=F32)


def softplus(z):
    return jnp.maximum(z, 0.0) + jnp.log1p(jnp.exp(-jnp.abs(z)))


def pick(condition, value=1.0):
    return jnp.where(condition, value, 0.0).astype(F32)


def owner_of(index, height):
    return ((index >> height) << height) + (1 << (height - 1))


def xor_lanes(x, slot, bit):
    step = 8 * bit
    if step == 64:
        return pltpu.roll(x, 64, 1)
    return jnp.where((slot & bit) != 0, pltpu.roll(x, step, 1), pltpu.roll(x, 128 - step, 1))


def xor_rows(x, bit):
    if bit >= 8:
        far = bit // 8
        return jnp.concatenate([x[i ^ far : (i ^ far) + 1] for i in range(4)], axis=0)
    if bit == 4:
        return pltpu.roll(x, 4, 1)
    odd = (iota((4, 8, 128), 1) & bit) != 0
    return jnp.where(odd, pltpu.roll(x, bit, 1), pltpu.roll(x, 8 - bit, 1))


def total(x):
    y = (x[0] + x[1]) + (x[2] + x[3])
    for step in (4, 2, 1):
        y = y + pltpu.roll(y, step, 0)
    for step in (64, 32, 16, 8):
        y = y + pltpu.roll(y, step, 1)
    return y


def kernel(
    lf_in, nf_in, w_in_in, w_out_in, leaf_var_in, node_var_in, inner_var_in, sub_sizes_in,
    x_out, r_out,
    lf, nf, w_in, w_out, leaf_var, node_var, inner_var, sub_sizes, v_buf, w_low, w_top, send1, recv1, send2, recv2, send3, recv3, rows_buf,
    lf_sems, in_sems, ss1, rs1, ss2, rs2, ss3, rs3,
):
    g = lax.axis_index("grp")
    b = lax.axis_index("basin")
    q = g * BASIN + b
    each = 16 // CHUNKS
    pairs = (
        (w_in_in, w_in), (nf_in, nf), (w_out_in, w_out), (sub_sizes_in, sub_sizes),
        (node_var_in, node_var), (leaf_var_in, leaf_var), (inner_var_in, inner_var),
    )
    first = [pltpu.make_async_copy(a, c, in_sems.at[k]) for k, (a, c) in enumerate(pairs)]
    loads = [
        pltpu.make_async_copy(lf_in.at[pl.ds(each * c, each)], lf.at[pl.ds(each * c, each)], lf_sems.at[c])
        for c in range(CHUNKS)
    ]
    for load in first + loads:
        load.start()
    barrier = pltpu.get_barrier_semaphore()
    for step in range(1, GRP):
        pl.semaphore_signal(barrier, inc=1, device_id=(lax.rem(g + step, GRP), b), device_id_type=MESH)
    for step in range(1, BASIN):
        pl.semaphore_signal(barrier, inc=1, device_id=(g, lax.rem(b + step, BASIN)), device_id_type=MESH)

    for load in first:
        load.wait()

    half = w_in[...] * jnp.asarray(0.5, BF16)
    eight = jnp.concatenate([w_out[...].astype(F32), jnp.zeros((1, 512), F32)], axis=0)
    out_all = jnp.concatenate([eight] * 16, axis=0).astype(BF16)

    def network(features):
        h = lax.dot_general(features, half, (((1,), (1,)), ((), ())), preferred_element_type=F32)
        hidden = (h + h * jnp.tanh(h)).astype(BF16)
        return lax.dot_general(hidden, out_all, (((1,), (1,)), ((), ())), preferred_element_type=F32)

    zn = network(nf[...].reshape(176, 128)).reshape(11, 16, 128)
    member3 = (iota((11, 16, 128), 2) >> 3) == iota((11, 16, 128), 1)
    zn = jnp.sum(jnp.where(member3, zn, 0.0), axis=1)
    soft_up = softplus(jnp.concatenate([zn, jnp.zeros((5, 128), F32)], axis=0))

    leaf_row = iota((1, 128), 1)
    leaf_i = iota((128, 128), 0)
    leaf_j = iota((128, 128), 1)
    label_row = jnp.zeros((1, 128), jnp.int32)
    label_i = jnp.zeros((128, 128), jnp.int32)
    end = jnp.int32(0)
    for s in range(9):
        end = end + sub_sizes[0, s]
        label_row = label_row + (leaf_row >= end).astype(jnp.int32)
        label_i = label_i + (leaf_i >= end).astype(jnp.int32)
    scale_row = jnp.zeros((1, 128), F32)
    one_row = jnp.ones((1, 128), F32)
    node16 = iota((16, 128), 0)
    node_inv = jnp.zeros((16, 128), F32)
    for s in range(9):
        var = node_var[0, s] * one_row
        scale_row = jnp.where(label_row == s, 1.0 / (sub_sizes[0, s].astype(F32) * var), scale_row)
        node_inv = jnp.where(node16 == s, 1.0 / var, node_inv)
    dev_var = node_var[0, 9] * one_row
    node_inv = jnp.where(node16 == 9, 1.0 / dev_var, node_inv)
    leaf_inv = 1.0 / leaf_var[...]
    op1 = (
        jnp.where(label_i == label_row, scale_row, 0.0)
        + 1.0 / (LEAF * dev_var)
        + jnp.where(leaf_i == leaf_j, leaf_inv, 0.0)
    )
    op2 = exact_dot(op1, op1)
    op3 = exact_dot(op2, op1)
    n1 = jnp.sum(op1, axis=0, keepdims=True)
    n2 = jnp.sum(op2, axis=0, keepdims=True)
    n3 = jnp.sum(op3, axis=0, keepdims=True)
    row8 = iota((8, 128), 0)
    low = jnp.where(row8 == 0, one_row, jnp.where(row8 == 1, n1, jnp.where(row8 == 2, n2, 0.0)))
    high = exact_dot(low, op3)
    n4 = high[1:2]
    n5 = high[2:3]
    powers = (one_row, n1, n2, n3, n4, n5)
    to_m = jnp.where(node16 == 0, one_row, 0.0)
    to_n = jnp.zeros((8, 128), F32)
    for k in range(1, 6):
        to_m = jnp.where(node16 == 16 - k, powers[k], to_m)
        to_n = jnp.where(row8 == k - 1, powers[k], to_n)
    lane8 = iota((8, 128), 1)
    n_col = jnp.sum(to_n, axis=1, keepdims=True)
    n_lanes = jnp.sum(jnp.where((lane8 & 7) == row8, n_col, 0.0), axis=0, keepdims=True)
    leaf_inv_col = jnp.sum(jnp.where(leaf_i == leaf_j, leaf_inv, 0.0), axis=1, keepdims=True)
    table = pick((leaf_j == label_i) | (leaf_j == 9))[:, :16]
    inner_row = inner_var[...]
    inner_at = iota((1, 511), 1)
    own_var = jnp.sum(jnp.where(inner_at == jnp.maximum(q - 1, 0), inner_row, 0.0), axis=1, keepdims=True)
    own_gain = jnp.where(q >= 1, 1.0 / own_var, 0.0)
    upper = exact_dot(table, soft_up * node_inv)

    lanes = leaf_j
    z = jnp.zeros((128, 128), F32)
    for c in range(CHUNKS):
        loads[c].wait()
        for m in range(each * c, each * c + each):
            z = jnp.where((lanes >> 3) == m, network(lf[m].T), z)
    b0 = softplus(z) * leaf_inv_col + upper
    v1 = exact_dot(op1, b0)
    v2 = exact_dot(op2, b0)
    v3 = exact_dot(op3, b0)
    v_buf[0] = b0
    v_buf[1] = v1
    v_buf[2] = v2
    v_buf[3] = v3

    figures = exact_dot(to_m, b0)
    figures = jnp.where(node16 == 10, n_lanes, figures)
    figures = jnp.where(node16 == 16 - INNER, soft_up[10:11] * own_gain, figures)
    products = (b0 * b0, b0 * v1, v1 * v1, v1 * v2, v2 * v2, v2 * v3)
    for k in range(6):
        figures = jnp.where(node16 == 8 - k, jnp.sum(products[k], axis=0, keepdims=True), figures)
    send1[...] = turn_out(figures).reshape(16, 1, 128)

    pl.semaphore_wait(barrier, GRP + BASIN - 2)

    for offset in far_first((8, 2)):
        to = peer(g, offset, (8, 2))
        pltpu.make_async_remote_copy(
            src_ref=send1.at[lax.rem(16 - to, 16)], dst_ref=recv1.at[g], send_sem=ss1, recv_sem=rs1,
            device_id=(to, b), device_id_type=MESH,
        ).start()
    recv1[pl.ds(g, 1)] = send1[pl.ds(lax.rem(16 - g, 16), 1)]

    at = iota((32, 511), 1) + 1
    spread = jnp.where((at & 31) == iota((32, 511), 0), inner_row, 0.0)
    at_col = iota((511, 128), 0) + 1
    to_slot = pick((at_col >> 5) == (iota((511, 128), 1) >> 3))
    var_of = exact_dot(spread, to_slot)
    low_row = iota((32, 32), 0)
    low_col = iota((32, 32), 1)
    row32 = iota((32, 128), 0)
    lane32 = iota((32, 128), 1)
    inverse = jnp.where((row32 == 0) & (lane32 < 8), 0.0, 1.0 / jnp.where((row32 == 0) & (lane32 < 8), 1.0, var_of))
    low_all = jnp.zeros((32, 32), F32)
    for h in range(1, 6):
        chosen = pick(low_col == owner_of(low_row, h))
        low_all = low_all + chosen
        w_low[h - 1] = exact_dot(chosen, inverse) * (1.0 / (LEAF * 2**h))
    from_lane = iota((128, 128), 0)
    top_all = jnp.zeros((128, 128), F32)
    same_day = (from_lane & 7) == (lanes & 7)
    for h in range(1, 5):
        chosen = pick(same_day & ((from_lane >> 3) == owner_of(lanes >> 3, h)))
        top_all = top_all + chosen
        w_top[h - 1] = exact_dot(jnp.broadcast_to(inverse[0:1], (8, 128)), chosen) * (1.0 / (LEAF * 2 ** (h + 5)))
    pad8 = (lane8 & 7) == 7
    to_pad = pick(((lanes & 7) == 7) & ((from_lane & 7) == (lanes >> 3)) & ((lanes >> 3) < 7))
    from_pad = pick(((from_lane & 7) == 7) & ((lanes & 7) == (from_lane >> 3)) & ((from_lane >> 3) < 7))
    same_slot = (from_lane >> 3) == (lanes >> 3)
    to_n_lanes = jnp.concatenate([pick(same_slot & ((from_lane & 7) == k)) for k in range(5)], axis=1)

    pltpu.make_async_copy(recv1.at[pl.ds(0, GRP - 1)], recv1.at[pl.ds(0, GRP - 1)], rs1).wait()
    turned = turn_in(recv1[...].reshape(16, 128), g)
    sums = exact_dot(turned[8:16], to_pad)
    send2[...] = jnp.where(pad8, sums, turned[:8])

    for offset in far_first((8, 4)):
        to = peer(b, offset, (8, 4))
        pltpu.make_async_remote_copy(
            src_ref=send2, dst_ref=recv2.at[b], send_sem=ss2, recv_sem=rs2,
            device_id=(g, to), device_id_type=MESH,
        ).start()
    recv2[pl.ds(b, 1)] = send2[...][None]
    pltpu.make_async_copy(recv2.at[pl.ds(0, BASIN - 1)], recv2.at[pl.ds(0, BASIN - 1)], rs2).wait()

    everything = recv2[...]
    fluct = exact_dot(jnp.sum(everything, axis=0), from_pad)
    p = [jnp.broadcast_to(fluct[k : k + 1], (8, 128)) for k in range(6)]
    own = recv2[:, INNER, :]
    m = [recv2[:, k, :].reshape(4, 8, 128) for k in range(6)]
    n_all = exact_dot(recv2[:, 6, :], to_n_lanes)
    n = [F32(LEAF)] + [n_all[:, 128 * k : 128 * k + 128].reshape(4, 8, 128) for k in range(5)]
    rho = exact_dot(low_all, own) + exact_dot(jnp.broadcast_to(own[0:1], (8, 128)), top_all)[0:1]
    rho = rho.reshape(4, 8, 128)
    slot8 = lane8 >> 3

    def inner(s):
        y = s
        u = jnp.zeros_like(s)
        for h in range(5):
            y = y + xor_rows(y, 1 << h)
            u = u + w_low[h].reshape(4, 8, 128) * y
        t = y[0]
        top = jnp.zeros((8, 128), F32)
        for h in range(4):
            t = t + xor_lanes(t, slot8, 1 << h)
            top = top + w_top[h] * t
        return u + top[None]

    def combine(c, e, shift):
        out = 0.0
        for j in range(len(c)):
            out = out + c[j] * m[j + shift] + e[j] * n[j + shift]
        return out

    def form(c, e, shift):
        whole = 0.0
        each = 0.0
        for j in range(len(c)):
            for k in range(j, len(c)):
                twice = 1.0 if j == k else 2.0
                t = j + k + shift
                whole = whole + (twice * c[j] * c[k]) * p[t]
                cross = c[j] * e[k] if j == k else c[j] * e[k] + c[k] * e[j]
                each = each + 2.0 * cross * m[t] + (twice * e[j]) * e[k] * n[t]
        return whole, each

    one = jnp.ones((8, 128), F32)
    d_c = [one]
    d_e = [rho]
    r_c = [one]
    r_e = [rho]
    whole, each = form(d_c, d_e, 0)
    norm = whole + total(each)
    rows_buf[0] = rho.reshape(32, 128)
    steps = []
    betas = []
    for it in range(3):
        s = combine(d_c, d_e, 0)
        image = inner(s)
        rows_buf[it + 1] = image.reshape(32, 128)
        whole, each = form(d_c, d_e, 1)
        curvature = whole + total(each + s * image)
        alpha = norm / curvature
        steps.append(alpha)
        if it == 2:
            break
        whole, each = form(d_c, d_e, 2)
        square = whole + total(each + image * (2.0 * combine(d_c, d_e, 1) + LEAF * image))
        after = alpha * alpha * square - norm
        beta = after / norm
        betas.append(beta)
        r_c = [a - alpha * i for a, i in zip(r_c + [0.0], [0.0] + d_c)]
        r_e = [a - alpha * i for a, i in zip(r_e + [0.0], [image] + d_e)]
        d_c = [a + beta * i for a, i in zip(r_c, d_c + [0.0])]
        d_e = [a + beta * i for a, i in zip(r_e, d_e + [0.0])]
        norm = after

    mine = [rows_buf[k, pl.ds(b, 1), :] for k in range(4)]
    d_c = [one[0:1]]
    d_e = [mine[0]]
    r_c = [one[0:1]]
    r_e = [mine[0]]
    x_c = [0.0] * 3
    x_e = [0.0] * 3
    for it in range(3):
        alpha = steps[it][0:1]
        for k in range(it + 1):
            x_c[k] = x_c[k] + alpha * d_c[k]
            x_e[k] = x_e[k] + alpha * d_e[k]
        r_c = [a - alpha * i for a, i in zip(r_c + [0.0], [0.0] + d_c)]
        r_e = [a - alpha * i for a, i in zip(r_e + [0.0], [mine[it + 1]] + d_e)]
        if it < 2:
            beta = betas[it][0:1]
            d_c = [a + beta * i for a, i in zip(r_c, d_c + [0.0])]
            d_e = [a + beta * i for a, i in zip(r_e, d_e + [0.0])]
    spare = jnp.zeros((1, 128), F32)
    values = r_e + x_e + [spare] + r_c[1:] + x_c + [spare, spare]
    back = jnp.concatenate([values[(16 - k) % 16] for k in range(16)], axis=0)
    send3[...] = turn_out(back).reshape(16, 1, 128)

    for offset in far_first((8, 2)):
        to = peer(g, offset, (8, 2))
        pltpu.make_async_remote_copy(
            src_ref=send3.at[lax.rem(16 - to, 16)], dst_ref=recv3.at[g], send_sem=ss3, recv_sem=rs3,
            device_id=(to, b), device_id_type=MESH,
        ).start()
    recv3[pl.ds(g, 1)] = send3[pl.ds(lax.rem(16 - g, 16), 1)]
    lift_r = jnp.zeros((128, 128), F32)
    lift_x = jnp.zeros((128, 128), F32)
    for k in range(4):
        lift_r = jnp.where(leaf_i == k, powers[k], lift_r)
        if k < 3:
            lift_x = jnp.where(leaf_i == 4 + k, powers[k], lift_x)
    lift = jnp.concatenate([lift_r.T[:, :16], lift_x.T[:, :16]], axis=0)
    pltpu.make_async_copy(recv3.at[pl.ds(0, GRP - 1)], recv3.at[pl.ds(0, GRP - 1)], rs3).wait()
    gains = turn_in(recv3[...].reshape(16, 128), g)
    gains = jnp.where((iota((16, 128), 1) & 7) == 7, 0.0, gains)
    lifted = exact_dot(lift, gains)
    r = lifted[:128] + v_buf[0]
    x = lifted[128:]
    for k in range(3):
        r = r + gains[8 + k : 9 + k] * v_buf[k + 1]
        x = x + gains[11 + k : 12 + k] * v_buf[k]
    x = x.T
    r = r.T
    for k in range(16):
        x_out[7 * k : 7 * k + 7, :] = x[8 * k : 8 * k + 7]
        r_out[7 * k : 7 * k + 7, :] = r[8 * k : 8 * k + 7]

    pltpu.make_async_copy(recv1.at[pl.ds(0, GRP - 1)], recv1.at[pl.ds(0, GRP - 1)], ss1).wait()
    pltpu.make_async_copy(recv2.at[pl.ds(0, BASIN - 1)], recv2.at[pl.ds(0, BASIN - 1)], ss2).wait()
    pltpu.make_async_copy(recv3.at[pl.ds(0, GRP - 1)], recv3.at[pl.ds(0, GRP - 1)], ss3).wait()


def on_device(leaf_features, node_features, w_in, w_out, leaf_var, node_var, inner_var, sub_sizes):
    vmem = pl.BlockSpec(memory_space=pltpu.VMEM)
    hbm = pl.BlockSpec(memory_space=pltpu.HBM)
    tile = jax.ShapeDtypeStruct((112, 128), F32)
    return pl.pallas_call(
        kernel,
        out_shape=(tile, tile),
        in_specs=[hbm] * 8,
        out_specs=(vmem, vmem),
        scratch_shapes=[
            pltpu.VMEM((16, 128, 128), BF16),
            pltpu.VMEM((11, 16, 128), BF16),
            pltpu.VMEM((512, 128), BF16),
            pltpu.VMEM((7, 512), BF16),
            pltpu.VMEM((1, 128), F32),
            pltpu.SMEM((1, 10), F32),
            pltpu.VMEM((1, 511), F32),
            pltpu.SMEM((1, 9), jnp.int32),
            pltpu.VMEM((4, 128, 128), F32),
            pltpu.VMEM((5, 32, 128), F32),
            pltpu.VMEM((4, 8, 128), F32),
            pltpu.VMEM((16, 1, 128), F32),
            pltpu.VMEM((16, 1, 128), F32),
            pltpu.VMEM((8, 128), F32),
            pltpu.VMEM((32, 8, 128), F32),
            pltpu.VMEM((16, 1, 128), F32),
            pltpu.VMEM((16, 1, 128), F32),
            pltpu.VMEM((4, 32, 128), F32),
            pltpu.SemaphoreType.DMA((CHUNKS,)),
            pltpu.SemaphoreType.DMA((7,)),
        ]
        + [pltpu.SemaphoreType.DMA] * 6,
        compiler_params=pltpu.CompilerParams(collective_id=0, has_side_effects=True),
    )(
        leaf_features, jnp.transpose(node_features, (2, 0, 1)), w_in, w_out,
        leaf_var.reshape(1, -1), node_var.reshape(1, -1), inner_var.reshape(1, -1), sub_sizes,
    )


def solution(mesh):
    return jax.shard_map(
        on_device,
        mesh=mesh,
        in_specs=(
            P(None, None, ("grp", "basin")),
            P(None, None, ("grp", "basin")),
            P(),
            P(),
            P(("grp", "basin")),
            P(("grp", "basin")),
            P(),
            P(("grp", "basin"), None),
        ),
        out_specs=(P(None, ("grp", "basin")), P(None, ("grp", "basin"))),
        check_vma=False,
    )
```

```python
import jax
import jax.numpy as jnp
from jax import lax
from jax.experimental import pallas as pl
from jax.experimental.pallas import tpu as pltpu
from jax.sharding import PartitionSpec as P

MESH = pl.DeviceIdType.MESH
F32 = jnp.float32
BF16 = jnp.bfloat16
LEAF = 128
GRP = 16
BASIN = 32
INNER = 7
CHUNKS = 4


def iota(shape, axis):
    return lax.broadcasted_iota(jnp.int32, shape, axis)


def far_first(sizes):
    a, b = sizes
    offsets = [(i, j) for i in range(a) for j in range(b) if i or j]
    return sorted(offsets, key=lambda o: -(min(o[0], a - o[0]) + min(o[1], b - o[1])))


def peer(index, offset, sizes):
    a, b = sizes
    shift = b.bit_length() - 1
    slow = ((index >> shift) + offset[0]) & (a - 1)
    return (slow << shift) + ((index + offset[1]) & (b - 1))


def turn_out(x):
    y = pltpu.roll(x, 0, 1, stride=8, stride_axis=0)
    slot = iota((16, 128), 1) >> 3
    for k in (1, 2, 4, 8):
        y = jnp.where((slot & k) != 0, pltpu.roll(y, 16 - k, 0), y)
    return y


def turn_in(x, me):
    y = pltpu.roll(x, 0, 1, stride=8, stride_axis=0)
    away = (iota((16, 128), 1) >> 3) - me
    for k in (1, 2, 4, 8):
        y = jnp.where((away & k) != 0, pltpu.roll(y, 16 - k, 0), y)
    y = pltpu.roll(y, 0, 1, stride=8, stride_axis=0)
    return pltpu.roll(y, lax.rem(128 - 8 * me, 128), 1)


def exact_dot(a, b):
    return jnp.dot(a, b, precision=lax.Precision.HIGHEST, preferred_element_type=F32)


def softplus(z):
    return jnp.maximum(z, 0.0) + jnp.log1p(jnp.exp(-jnp.abs(z)))


def pick(condition, value=1.0):
    return jnp.where(condition, value, 0.0).astype(F32)


def owner_of(index, height):
    return ((index >> height) << height) + (1 << (height - 1))


def xor_lanes(x, slot, bit):
    step = 8 * bit
    if step == 64:
        return pltpu.roll(x, 64, 1)
    return jnp.where((slot & bit) != 0, pltpu.roll(x, step, 1), pltpu.roll(x, 128 - step, 1))


def xor_rows(x, bit):
    if bit >= 8:
        far = bit // 8
        return jnp.concatenate([x[i ^ far : (i ^ far) + 1] for i in range(4)], axis=0)
    if bit == 4:
        return pltpu.roll(x, 4, 1)
    odd = (iota((4, 8, 128), 1) & bit) != 0
    return jnp.where(odd, pltpu.roll(x, bit, 1), pltpu.roll(x, 8 - bit, 1))


def total(x):
    y = (x[0] + x[1]) + (x[2] + x[3])
    for step in (4, 2, 1):
        y = y + pltpu.roll(y, step, 0)
    for step in (64, 32, 16, 8):
        y = y + pltpu.roll(y, step, 1)
    return y


def kernel(
    lf_in, nf_in, w_in_in, w_out_in, leaf_var_in, node_var_in, inner_var_in, sub_sizes_in,
    x_out, r_out,
    lf, nf, w_in, w_out, leaf_var, node_var, inner_var, sub_sizes, v_buf, w_low, w_top, send1, recv1, send2, recv2, send3, recv3, rows_buf,
    lf_sems, in_sems, ss1, rs1, ss2, rs2, ss3, rs3,
):
    g = lax.axis_index("grp")
    b = lax.axis_index("basin")
    q = g * BASIN + b
    each = 16 // CHUNKS
    pairs = (
        (w_in_in, w_in), (nf_in, nf), (w_out_in, w_out), (sub_sizes_in, sub_sizes),
        (node_var_in, node_var), (leaf_var_in, leaf_var), (inner_var_in, inner_var),
    )
    first = [pltpu.make_async_copy(a, c, in_sems.at[k]) for k, (a, c) in enumerate(pairs)]
    loads = [
        pltpu.make_async_copy(lf_in.at[pl.ds(each * c, each)], lf.at[pl.ds(each * c, each)], lf_sems.at[c])
        for c in range(CHUNKS)
    ]
    for load in first + loads:
        load.start()
    barrier = pltpu.get_barrier_semaphore()
    for step in range(1, GRP):
        pl.semaphore_signal(barrier, inc=1, device_id=(lax.rem(g + step, GRP), b), device_id_type=MESH)
    for step in range(1, BASIN):
        pl.semaphore_signal(barrier, inc=1, device_id=(g, lax.rem(b + step, BASIN)), device_id_type=MESH)

    for load in first:
        load.wait()

    half = w_in[...] * jnp.asarray(0.5, BF16)
    eight = jnp.concatenate([w_out[...].astype(F32), jnp.zeros((1, 512), F32)], axis=0)
    out_all = jnp.concatenate([eight] * 16, axis=0).astype(BF16)

    def network(features):
        h = lax.dot_general(features, half, (((1,), (1,)), ((), ())), preferred_element_type=F32)
        hidden = (h + h * jnp.tanh(h)).astype(BF16)
        return lax.dot_general(hidden, out_all, (((1,), (1,)), ((), ())), preferred_element_type=F32)

    zn = network(nf[...].reshape(176, 128)).reshape(11, 16, 128)
    member3 = (iota((11, 16, 128), 2) >> 3) == iota((11, 16, 128), 1)
    zn = jnp.sum(jnp.where(member3, zn, 0.0), axis=1)
    soft_up = softplus(jnp.concatenate([zn, jnp.zeros((5, 128), F32)], axis=0))

    leaf_row = iota((1, 128), 1)
    leaf_i = iota((128, 128), 0)
    leaf_j = iota((128, 128), 1)
    label_row = jnp.zeros((1, 128), jnp.int32)
    label_i = jnp.zeros((128, 128), jnp.int32)
    end = jnp.int32(0)
    for s in range(9):
        end = end + sub_sizes[0, s]
        label_row = label_row + (leaf_row >= end).astype(jnp.int32)
        label_i = label_i + (leaf_i >= end).astype(jnp.int32)
    scale_row = jnp.zeros((1, 128), F32)
    one_row = jnp.ones((1, 128), F32)
    node16 = iota((16, 128), 0)
    node_inv = jnp.zeros((16, 128), F32)
    for s in range(9):
        var = node_var[0, s] * one_row
        scale_row = jnp.where(label_row == s, 1.0 / (sub_sizes[0, s].astype(F32) * var), scale_row)
        node_inv = jnp.where(node16 == s, 1.0 / var, node_inv)
    dev_var = node_var[0, 9] * one_row
    node_inv = jnp.where(node16 == 9, 1.0 / dev_var, node_inv)
    leaf_inv = 1.0 / leaf_var[...]
    op1 = (
        jnp.where(label_i == label_row, scale_row, 0.0)
        + 1.0 / (LEAF * dev_var)
        + jnp.where(leaf_i == leaf_j, leaf_inv, 0.0)
    )
    op2 = exact_dot(op1, op1)
    op3 = exact_dot(op2, op1)
    n1 = jnp.sum(op1, axis=0, keepdims=True)
    n2 = jnp.sum(op2, axis=0, keepdims=True)
    n3 = jnp.sum(op3, axis=0, keepdims=True)
    row8 = iota((8, 128), 0)
    low = jnp.where(row8 == 0, one_row, jnp.where(row8 == 1, n1, jnp.where(row8 == 2, n2, 0.0)))
    high = exact_dot(low, op3)
    n4 = high[1:2]
    n5 = high[2:3]
    powers = (one_row, n1, n2, n3, n4, n5)
    to_m = jnp.where(node16 == 0, one_row, 0.0)
    to_n = jnp.zeros((8, 128), F32)
    for k in range(1, 6):
        to_m = jnp.where(node16 == 16 - k, powers[k], to_m)
        to_n = jnp.where(row8 == k - 1, powers[k], to_n)
    lane8 = iota((8, 128), 1)
    n_col = jnp.sum(to_n, axis=1, keepdims=True)
    n_lanes = jnp.sum(jnp.where((lane8 & 7) == row8, n_col, 0.0), axis=0, keepdims=True)
    leaf_inv_col = jnp.sum(jnp.where(leaf_i == leaf_j, leaf_inv, 0.0), axis=1, keepdims=True)
    table = pick((leaf_j == label_i) | (leaf_j == 9))[:, :16]
    inner_row = inner_var[...]
    inner_at = iota((1, 511), 1)
    own_var = jnp.sum(jnp.where(inner_at == jnp.maximum(q - 1, 0), inner_row, 0.0), axis=1, keepdims=True)
    own_gain = jnp.where(q >= 1, 1.0 / own_var, 0.0)
    upper = exact_dot(table, soft_up * node_inv)

    lanes = leaf_j
    z = jnp.zeros((128, 128), F32)
    for c in range(CHUNKS):
        loads[c].wait()
        for m in range(each * c, each * c + each):
            z = jnp.where((lanes >> 3) == m, network(lf[m].T), z)
    b0 = softplus(z) * leaf_inv_col + upper
    v1 = exact_dot(op1, b0)
    v2 = exact_dot(op2, b0)
    v3 = exact_dot(op3, b0)
    v_buf[0] = b0
    v_buf[1] = v1
    v_buf[2] = v2
    v_buf[3] = v3

    figures = exact_dot(to_m, b0)
    figures = jnp.where(node16 == 10, n_lanes, figures)
    figures = jnp.where(node16 == 16 - INNER, soft_up[10:11] * own_gain, figures)
    products = (b0 * b0, b0 * v1, v1 * v1, v1 * v2, v2 * v2, v2 * v3)
    for k in range(6):
        figures = jnp.where(node16 == 8 - k, jnp.sum(products[k], axis=0, keepdims=True), figures)
    send1[...] = turn_out(figures).reshape(16, 1, 128)

    pl.semaphore_wait(barrier, GRP + BASIN - 2)

    for offset in far_first((8, 2)):
        to = peer(g, offset, (8, 2))
        pltpu.make_async_remote_copy(
            src_ref=send1.at[lax.rem(16 - to, 16)], dst_ref=recv1.at[g], send_sem=ss1, recv_sem=rs1,
            device_id=(to, b), device_id_type=MESH,
        ).start()
    recv1[pl.ds(g, 1)] = send1[pl.ds(lax.rem(16 - g, 16), 1)]

    at = iota((32, 511), 1) + 1
    spread = jnp.where((at & 31) == iota((32, 511), 0), inner_row, 0.0)
    at_col = iota((511, 128), 0) + 1
    to_slot = pick((at_col >> 5) == (iota((511, 128), 1) >> 3))
    var_of = exact_dot(spread, to_slot)
    low_row = iota((32, 32), 0)
    low_col = iota((32, 32), 1)
    row32 = iota((32, 128), 0)
    lane32 = iota((32, 128), 1)
    inverse = jnp.where((row32 == 0) & (lane32 < 8), 0.0, 1.0 / jnp.where((row32 == 0) & (lane32 < 8), 1.0, var_of))
    low_all = jnp.zeros((32, 32), F32)
    for h in range(1, 6):
        chosen = pick(low_col == owner_of(low_row, h))
        low_all = low_all + chosen
        w_low[h - 1] = exact_dot(chosen, inverse) * (1.0 / (LEAF * 2**h))
    from_lane = iota((128, 128), 0)
    top_all = jnp.zeros((128, 128), F32)
    same_day = (from_lane & 7) == (lanes & 7)
    for h in range(1, 5):
        chosen = pick(same_day & ((from_lane >> 3) == owner_of(lanes >> 3, h)))
        top_all = top_all + chosen
        w_top[h - 1] = exact_dot(jnp.broadcast_to(inverse[0:1], (8, 128)), chosen) * (1.0 / (LEAF * 2 ** (h + 5)))
    pad8 = (lane8 & 7) == 7
    to_pad = pick(((lanes & 7) == 7) & ((from_lane & 7) == (lanes >> 3)) & ((lanes >> 3) < 7))
    from_pad = pick(((from_lane & 7) == 7) & ((lanes & 7) == (from_lane >> 3)) & ((from_lane >> 3) < 7))
    same_slot = (from_lane >> 3) == (lanes >> 3)
    to_n_lanes = jnp.concatenate([pick(same_slot & ((from_lane & 7) == k)) for k in range(5)], axis=1)

    pltpu.make_async_copy(recv1.at[pl.ds(0, GRP - 1)], recv1.at[pl.ds(0, GRP - 1)], rs1).wait()
    turned = turn_in(recv1[...].reshape(16, 128), g)
    sums = exact_dot(turned[8:16], to_pad)
    send2[...] = jnp.where(pad8, sums, turned[:8])

    for offset in far_first((8, 4)):
        to = peer(b, offset, (8, 4))
        pltpu.make_async_remote_copy(
            src_ref=send2, dst_ref=recv2.at[b], send_sem=ss2, recv_sem=rs2,
            device_id=(g, to), device_id_type=MESH,
        ).start()
    recv2[pl.ds(b, 1)] = send2[...][None]
    pltpu.make_async_copy(recv2.at[pl.ds(0, BASIN - 1)], recv2.at[pl.ds(0, BASIN - 1)], rs2).wait()

    everything = recv2[...]
    fluct = exact_dot(jnp.sum(everything, axis=0), from_pad)
    p = [jnp.broadcast_to(fluct[k : k + 1], (8, 128)) for k in range(6)]
    own = recv2[:, INNER, :]
    m = [recv2[:, k, :].reshape(4, 8, 128) for k in range(6)]
    n_all = exact_dot(recv2[:, 6, :], to_n_lanes)
    n = [F32(LEAF)] + [n_all[:, 128 * k : 128 * k + 128].reshape(4, 8, 128) for k in range(5)]
    rho = exact_dot(low_all, own) + exact_dot(jnp.broadcast_to(own[0:1], (8, 128)), top_all)[0:1]
    rho = rho.reshape(4, 8, 128)
    slot8 = lane8 >> 3

    def inner(s):
        y = s
        u = jnp.zeros_like(s)
        for h in range(5):
            y = y + xor_rows(y, 1 << h)
            u = u + w_low[h].reshape(4, 8, 128) * y
        t = y[0]
        top = jnp.zeros((8, 128), F32)
        for h in range(4):
            t = t + xor_lanes(t, slot8, 1 << h)
            top = top + w_top[h] * t
        return u + top[None]

    parts = [rho]
    sums = []
    for j in range(3):
        s = m[j]
        for k in range(j + 1):
            s = s + n[k] * parts[j - k]
        sums.append(s)
        parts.append(inner(s))
        rows_buf[j] = parts[j].reshape(32, 128)
    rows_buf[3] = parts[3].reshape(32, 128)

    def spread_of(c, u):
        return [sum(c[j] * u[j - k] for j in range(k, len(c))) for k in range(len(c))]

    def form(c, e, shift):
        whole = 0.0
        each = 0.0
        for j in range(len(c)):
            for k in range(j, len(c)):
                twice = 1.0 if j == k else 2.0
                t = j + k + shift
                whole = whole + (twice * c[j] * c[k]) * p[t]
                cross = c[j] * e[k] if j == k else c[j] * e[k] + c[k] * e[j]
                each = each + 2.0 * cross * m[t] + (twice * e[j]) * e[k] * n[t]
        return whole, each

    one = jnp.ones((8, 128), F32)
    d_c = [one]
    r_c = [one]
    x_c = [0.0, 0.0, 0.0]
    whole, each = form(d_c, [rho], 0)
    norm = whole + total(each)
    for it in range(3):
        d_e = spread_of(d_c, parts)
        image = sum(d_c[j] * parts[j + 1] for j in range(it + 1))
        whole, each = form(d_c, d_e, 1)
        curvature = whole + total(each + image * sum(d_c[j] * sums[j] for j in range(it + 1)))
        alpha = norm / curvature
        for k in range(it + 1):
            x_c[k] = x_c[k] + alpha * d_c[k]
        r_c = [a - alpha * i for a, i in zip(r_c + [0.0], [0.0] + d_c)]
        if it == 2:
            break
        whole, each = form(d_c, d_e, 2)
        along = sum(d_c[j] * m[j + 1] + d_e[j] * n[j + 1] for j in range(it + 1))
        square = whole + total(each + image * (2.0 * along + LEAF * image))
        after = alpha * alpha * square - norm
        beta = after / norm
        d_c = [a + beta * i for a, i in zip(r_c, d_c + [0.0])]
        norm = after

    mine = [rows_buf[k, pl.ds(b, 1), :] for k in range(4)]
    r_c = [c[0:1] for c in r_c]
    x_c = [c[0:1] for c in x_c]
    r_e = spread_of(r_c, mine)
    x_e = spread_of(x_c, mine)
    spare = jnp.zeros((1, 128), F32)
    values = r_e + x_e + [spare] + r_c[1:] + x_c + [spare, spare]
    back = jnp.concatenate([values[(16 - k) % 16] for k in range(16)], axis=0)
    send3[...] = turn_out(back).reshape(16, 1, 128)

    for offset in far_first((8, 2)):
        to = peer(g, offset, (8, 2))
        pltpu.make_async_remote_copy(
            src_ref=send3.at[lax.rem(16 - to, 16)], dst_ref=recv3.at[g], send_sem=ss3, recv_sem=rs3,
            device_id=(to, b), device_id_type=MESH,
        ).start()
    recv3[pl.ds(g, 1)] = send3[pl.ds(lax.rem(16 - g, 16), 1)]
    lift_r = jnp.zeros((128, 128), F32)
    lift_x = jnp.zeros((128, 128), F32)
    for k in range(4):
        lift_r = jnp.where(leaf_i == k, powers[k], lift_r)
        if k < 3:
            lift_x = jnp.where(leaf_i == 4 + k, powers[k], lift_x)
    lift = jnp.concatenate([lift_r.T[:, :16], lift_x.T[:, :16]], axis=0)
    pltpu.make_async_copy(recv3.at[pl.ds(0, GRP - 1)], recv3.at[pl.ds(0, GRP - 1)], rs3).wait()
    gains = turn_in(recv3[...].reshape(16, 128), g)
    gains = jnp.where((iota((16, 128), 1) & 7) == 7, 0.0, gains)
    lifted = exact_dot(lift, gains)
    r = lifted[:128] + v_buf[0]
    x = lifted[128:]
    for k in range(3):
        r = r + gains[8 + k : 9 + k] * v_buf[k + 1]
        x = x + gains[11 + k : 12 + k] * v_buf[k]
    x = x.T
    r = r.T
    for k in range(16):
        x_out[7 * k : 7 * k + 7, :] = x[8 * k : 8 * k + 7]
        r_out[7 * k : 7 * k + 7, :] = r[8 * k : 8 * k + 7]

    pltpu.make_async_copy(recv1.at[pl.ds(0, GRP - 1)], recv1.at[pl.ds(0, GRP - 1)], ss1).wait()
    pltpu.make_async_copy(recv2.at[pl.ds(0, BASIN - 1)], recv2.at[pl.ds(0, BASIN - 1)], ss2).wait()
    pltpu.make_async_copy(recv3.at[pl.ds(0, GRP - 1)], recv3.at[pl.ds(0, GRP - 1)], ss3).wait()


def on_device(leaf_features, node_features, w_in, w_out, leaf_var, node_var, inner_var, sub_sizes):
    vmem = pl.BlockSpec(memory_space=pltpu.VMEM)
    hbm = pl.BlockSpec(memory_space=pltpu.HBM)
    tile = jax.ShapeDtypeStruct((112, 128), F32)
    return pl.pallas_call(
        kernel,
        out_shape=(tile, tile),
        in_specs=[hbm] * 8,
        out_specs=(vmem, vmem),
        scratch_shapes=[
            pltpu.VMEM((16, 128, 128), BF16),
            pltpu.VMEM((11, 16, 128), BF16),
            pltpu.VMEM((512, 128), BF16),
            pltpu.VMEM((7, 512), BF16),
            pltpu.VMEM((1, 128), F32),
            pltpu.SMEM((1, 10), F32),
            pltpu.VMEM((1, 511), F32),
            pltpu.SMEM((1, 9), jnp.int32),
            pltpu.VMEM((4, 128, 128), F32),
            pltpu.VMEM((5, 32, 128), F32),
            pltpu.VMEM((4, 8, 128), F32),
            pltpu.VMEM((16, 1, 128), F32),
            pltpu.VMEM((16, 1, 128), F32),
            pltpu.VMEM((8, 128), F32),
            pltpu.VMEM((32, 8, 128), F32),
            pltpu.VMEM((16, 1, 128), F32),
            pltpu.VMEM((16, 1, 128), F32),
            pltpu.VMEM((4, 32, 128), F32),
            pltpu.SemaphoreType.DMA((CHUNKS,)),
            pltpu.SemaphoreType.DMA((7,)),
        ]
        + [pltpu.SemaphoreType.DMA] * 6,
        compiler_params=pltpu.CompilerParams(collective_id=0, has_side_effects=True, vmem_limit_bytes=32 * 1024 * 1024),
    )(*[
        pltpu.with_memory_space_constraint(a, pltpu.HBM)
        for a in (
            leaf_features, jnp.transpose(node_features, (2, 0, 1)), w_in, w_out,
            leaf_var.reshape(1, -1), node_var.reshape(1, -1), inner_var.reshape(1, -1), sub_sizes,
        )
    ])


def solution(mesh):
    return jax.shard_map(
        on_device,
        mesh=mesh,
        in_specs=(
            P(None, None, ("grp", "basin")),
            P(None, None, ("grp", "basin")),
            P(),
            P(),
            P(("grp", "basin")),
            P(("grp", "basin")),
            P(),
            P(("grp", "basin"), None),
        ),
        out_specs=(P(None, ("grp", "basin")), P(None, ("grp", "basin"))),
        check_vma=False,
    )
```

```python
import jax
import jax.numpy as jnp
from jax import lax
from jax.experimental import pallas as pl
from jax.experimental.pallas import tpu as pltpu
from jax.sharding import PartitionSpec as P

MESH = pl.DeviceIdType.MESH
F32 = jnp.float32
BF16 = jnp.bfloat16
LEAF = 128
GRP = 16
BASIN = 32
INNER = 7
CHUNKS = 4


def iota(shape, axis):
    return lax.broadcasted_iota(jnp.int32, shape, axis)


def far_first(sizes):
    a, b = sizes
    offsets = [(i, j) for i in range(a) for j in range(b) if i or j]
    return sorted(offsets, key=lambda o: -(min(o[0], a - o[0]) + min(o[1], b - o[1])))


def peer(index, offset, sizes):
    a, b = sizes
    shift = b.bit_length() - 1
    slow = ((index >> shift) + offset[0]) & (a - 1)
    return (slow << shift) + ((index + offset[1]) & (b - 1))


def turn_out(x):
    y = pltpu.roll(x, 0, 1, stride=8, stride_axis=0)
    slot = iota((16, 128), 1) >> 3
    for k in (1, 2, 4, 8):
        y = jnp.where((slot & k) != 0, pltpu.roll(y, 16 - k, 0), y)
    return y


def turn_in(x, me):
    y = pltpu.roll(x, 0, 1, stride=8, stride_axis=0)
    away = (iota((16, 128), 1) >> 3) - me
    for k in (1, 2, 4, 8):
        y = jnp.where((away & k) != 0, pltpu.roll(y, 16 - k, 0), y)
    y = pltpu.roll(y, 0, 1, stride=8, stride_axis=0)
    return pltpu.roll(y, lax.rem(128 - 8 * me, 128), 1)


def exact_dot(a, b):
    return jnp.dot(a, b, precision=lax.Precision.HIGHEST, preferred_element_type=F32)


def softplus(z):
    return jnp.maximum(z, 0.0) + jnp.log1p(jnp.exp(-jnp.abs(z)))


def pick(condition, value=1.0):
    return jnp.where(condition, value, 0.0).astype(F32)


def owner_of(index, height):
    return ((index >> height) << height) + (1 << (height - 1))


def xor_lanes(x, slot, bit):
    step = 8 * bit
    if step == 64:
        return pltpu.roll(x, 64, 1)
    return jnp.where((slot & bit) != 0, pltpu.roll(x, step, 1), pltpu.roll(x, 128 - step, 1))


def xor_rows(x, bit):
    if bit >= 8:
        far = bit // 8
        return jnp.concatenate([x[i ^ far : (i ^ far) + 1] for i in range(4)], axis=0)
    if bit == 4:
        return pltpu.roll(x, 4, 1)
    odd = (iota((4, 8, 128), 1) & bit) != 0
    return jnp.where(odd, pltpu.roll(x, bit, 1), pltpu.roll(x, 8 - bit, 1))


def total(x):
    y = (x[0] + x[1]) + (x[2] + x[3])
    for step in (4, 2, 1):
        y = y + pltpu.roll(y, step, 0)
    for step in (64, 32, 16, 8):
        y = y + pltpu.roll(y, step, 1)
    return y


def kernel(
    lf_in, nf_in, w_in_in, w_out_in, leaf_var_in, node_var_in, inner_var_in, sub_sizes_in,
    x_out, r_out,
    lf, nf, w_in, w_out, leaf_var, node_var, inner_var, sub_sizes, v_buf, w_low, w_top, send1, recv1, send2, recv2, send3, recv3, rows_buf,
    lf_sems, in_sems, ss1, rs1, ss2, rs2, ss3, rs3,
):
    g = lax.axis_index("grp")
    b = lax.axis_index("basin")
    q = g * BASIN + b
    each = 16 // CHUNKS
    pairs = (
        (w_in_in, w_in), (nf_in, nf), (w_out_in, w_out), (sub_sizes_in, sub_sizes),
        (node_var_in, node_var), (leaf_var_in, leaf_var), (inner_var_in, inner_var),
    )
    first = [pltpu.make_async_copy(a, c, in_sems.at[k]) for k, (a, c) in enumerate(pairs)]
    loads = [
        pltpu.make_async_copy(lf_in.at[pl.ds(each * c, each)], lf.at[pl.ds(each * c, each)], lf_sems.at[c])
        for c in range(CHUNKS)
    ]
    for load in first + loads:
        load.start()
    barrier = pltpu.get_barrier_semaphore()
    for step in range(1, GRP):
        pl.semaphore_signal(barrier, inc=1, device_id=(lax.rem(g + step, GRP), b), device_id_type=MESH)
    for step in range(1, BASIN):
        pl.semaphore_signal(barrier, inc=1, device_id=(g, lax.rem(b + step, BASIN)), device_id_type=MESH)

    for load in first:
        load.wait()

    half = w_in[...] * jnp.asarray(0.5, BF16)
    eight = jnp.concatenate([w_out[...].astype(F32), jnp.zeros((1, 512), F32)], axis=0)
    out_all = jnp.concatenate([eight] * 16, axis=0).astype(BF16)

    def network(features):
        h = lax.dot_general(features, half, (((1,), (1,)), ((), ())), preferred_element_type=F32)
        hidden = (h + h * jnp.tanh(h)).astype(BF16)
        return lax.dot_general(hidden, out_all, (((1,), (1,)), ((), ())), preferred_element_type=F32)

    zn = network(nf[...].reshape(176, 128)).reshape(11, 16, 128)
    member3 = (iota((11, 16, 128), 2) >> 3) == iota((11, 16, 128), 1)
    zn = jnp.sum(jnp.where(member3, zn, 0.0), axis=1)
    soft_up = softplus(jnp.concatenate([zn, jnp.zeros((5, 128), F32)], axis=0))

    leaf_row = iota((1, 128), 1)
    leaf_i = iota((128, 128), 0)
    leaf_j = iota((128, 128), 1)
    label_row = jnp.zeros((1, 128), jnp.int32)
    label_i = jnp.zeros((128, 128), jnp.int32)
    end = jnp.int32(0)
    for s in range(9):
        end = end + sub_sizes[0, s]
        label_row = label_row + (leaf_row >= end).astype(jnp.int32)
        label_i = label_i + (leaf_i >= end).astype(jnp.int32)
    scale_row = jnp.zeros((1, 128), F32)
    one_row = jnp.ones((1, 128), F32)
    node16 = iota((16, 128), 0)
    node_inv = jnp.zeros((16, 128), F32)
    for s in range(9):
        var = node_var[0, s] * one_row
        scale_row = jnp.where(label_row == s, 1.0 / (sub_sizes[0, s].astype(F32) * var), scale_row)
        node_inv = jnp.where(node16 == s, 1.0 / var, node_inv)
    dev_var = node_var[0, 9] * one_row
    node_inv = jnp.where(node16 == 9, 1.0 / dev_var, node_inv)
    leaf_inv = 1.0 / leaf_var[...]
    op1 = (
        jnp.where(label_i == label_row, scale_row, 0.0)
        + 1.0 / (LEAF * dev_var)
        + jnp.where(leaf_i == leaf_j, leaf_inv, 0.0)
    )
    op2 = exact_dot(op1, op1)
    op3 = exact_dot(op2, op1)
    n1 = jnp.sum(op1, axis=0, keepdims=True)
    n2 = jnp.sum(op2, axis=0, keepdims=True)
    n3 = jnp.sum(op3, axis=0, keepdims=True)
    row8 = iota((8, 128), 0)
    low = jnp.where(row8 == 0, one_row, jnp.where(row8 == 1, n1, jnp.where(row8 == 2, n2, 0.0)))
    high = exact_dot(low, op3)
    n4 = high[1:2]
    n5 = high[2:3]
    powers = (one_row, n1, n2, n3, n4, n5)
    to_m = jnp.where(node16 == 0, one_row, 0.0)
    to_n = jnp.zeros((8, 128), F32)
    for k in range(1, 6):
        to_m = jnp.where(node16 == 16 - k, powers[k], to_m)
        to_n = jnp.where(row8 == k - 1, powers[k], to_n)
    lane8 = iota((8, 128), 1)
    n_col = jnp.sum(to_n, axis=1, keepdims=True)
    n_lanes = jnp.sum(jnp.where((lane8 & 7) == row8, n_col, 0.0), axis=0, keepdims=True)
    leaf_inv_col = jnp.sum(jnp.where(leaf_i == leaf_j, leaf_inv, 0.0), axis=1, keepdims=True)
    table = pick((leaf_j == label_i) | (leaf_j == 9))[:, :16]
    inner_row = inner_var[...]
    inner_at = iota((1, 511), 1)
    own_var = jnp.sum(jnp.where(inner_at == jnp.maximum(q - 1, 0), inner_row, 0.0), axis=1, keepdims=True)
    own_gain = jnp.where(q >= 1, 1.0 / own_var, 0.0)
    upper = exact_dot(table, soft_up * node_inv)

    lanes = leaf_j
    z = jnp.zeros((128, 128), F32)
    for c in range(CHUNKS):
        loads[c].wait()
        for m in range(each * c, each * c + each):
            z = jnp.where((lanes >> 3) == m, network(lf[m].T), z)
    b0 = softplus(z) * leaf_inv_col + upper
    applied = exact_dot(jnp.concatenate([op1, op2, op3, to_m], axis=0), b0)
    v1 = applied[:128]
    v2 = applied[128:256]
    v3 = applied[256:384]
    v_buf[0] = b0
    v_buf[1] = v1
    v_buf[2] = v2
    v_buf[3] = v3

    figures = applied[384:]
    figures = jnp.where(node16 == 10, n_lanes, figures)
    figures = jnp.where(node16 == 16 - INNER, soft_up[10:11] * own_gain, figures)
    products = (b0 * b0, b0 * v1, v1 * v1, v1 * v2, v2 * v2, v2 * v3)
    for k in range(6):
        figures = jnp.where(node16 == 8 - k, jnp.sum(products[k], axis=0, keepdims=True), figures)
    send1[...] = turn_out(figures).reshape(16, 1, 128)

    pl.semaphore_wait(barrier, GRP + BASIN - 2)

    for offset in far_first((8, 2)):
        to = peer(g, offset, (8, 2))
        pltpu.make_async_remote_copy(
            src_ref=send1.at[lax.rem(16 - to, 16)], dst_ref=recv1.at[g], send_sem=ss1, recv_sem=rs1,
            device_id=(to, b), device_id_type=MESH,
        ).start()
    recv1[pl.ds(g, 1)] = send1[pl.ds(lax.rem(16 - g, 16), 1)]

    at = iota((32, 511), 1) + 1
    spread = jnp.where((at & 31) == iota((32, 511), 0), inner_row, 0.0)
    at_col = iota((511, 128), 0) + 1
    to_slot = pick((at_col >> 5) == (iota((511, 128), 1) >> 3))
    var_of = exact_dot(spread, to_slot)
    low_row = iota((32, 32), 0)
    low_col = iota((32, 32), 1)
    row32 = iota((32, 128), 0)
    lane32 = iota((32, 128), 1)
    inverse = jnp.where((row32 == 0) & (lane32 < 8), 0.0, 1.0 / jnp.where((row32 == 0) & (lane32 < 8), 1.0, var_of))
    low_all = jnp.zeros((32, 32), F32)
    for h in range(1, 6):
        chosen = pick(low_col == owner_of(low_row, h))
        low_all = low_all + chosen
        w_low[h - 1] = exact_dot(chosen, inverse) * (1.0 / (LEAF * 2**h))
    from_lane = iota((128, 128), 0)
    top_all = jnp.zeros((128, 128), F32)
    same_day = (from_lane & 7) == (lanes & 7)
    for h in range(1, 5):
        chosen = pick(same_day & ((from_lane >> 3) == owner_of(lanes >> 3, h)))
        top_all = top_all + chosen
        w_top[h - 1] = exact_dot(jnp.broadcast_to(inverse[0:1], (8, 128)), chosen) * (1.0 / (LEAF * 2 ** (h + 5)))
    pad8 = (lane8 & 7) == 7
    to_pad = pick(((lanes & 7) == 7) & ((from_lane & 7) == (lanes >> 3)) & ((lanes >> 3) < 7))
    from_pad = pick(((from_lane & 7) == 7) & ((lanes & 7) == (from_lane >> 3)) & ((from_lane >> 3) < 7))
    same_slot = (from_lane >> 3) == (lanes >> 3)
    to_n_lanes = jnp.concatenate([pick(same_slot & ((from_lane & 7) == k)) for k in range(5)], axis=1)

    pltpu.make_async_copy(recv1.at[pl.ds(0, GRP - 1)], recv1.at[pl.ds(0, GRP - 1)], rs1).wait()
    turned = turn_in(recv1[...].reshape(16, 128), g)
    sums = exact_dot(turned[8:16], to_pad)
    send2[...] = jnp.where(pad8, sums, turned[:8])

    for offset in far_first((8, 4)):
        to = peer(b, offset, (8, 4))
        pltpu.make_async_remote_copy(
            src_ref=send2, dst_ref=recv2.at[pl.ds(pl.multiple_of(8 * b, 8), 8)], send_sem=ss2, recv_sem=rs2,
            device_id=(g, to), device_id_type=MESH,
        ).start()
    recv2[pl.ds(pl.multiple_of(8 * b, 8), 8), :] = send2[...]
    pltpu.make_async_copy(recv2.at[pl.ds(0, 8 * (BASIN - 1))], recv2.at[pl.ds(0, 8 * (BASIN - 1))], rs2).wait()

    everything = recv2[...].reshape(32, 8, 128)
    fluct = exact_dot(jnp.sum(everything, axis=0), from_pad)
    p = [jnp.broadcast_to(fluct[k : k + 1], (8, 128)) for k in range(6)]
    own = recv2[pl.ds(INNER, 32, stride=8), :]
    m = [recv2[pl.ds(k, 32, stride=8), :].reshape(4, 8, 128) for k in range(6)]
    n_all = exact_dot(recv2[pl.ds(6, 32, stride=8), :], to_n_lanes)
    n = [F32(LEAF)] + [n_all[:, 128 * k : 128 * k + 128].reshape(4, 8, 128) for k in range(5)]
    rho = exact_dot(low_all, own) + exact_dot(jnp.broadcast_to(own[0:1], (8, 128)), top_all)[0:1]
    rho = rho.reshape(4, 8, 128)
    slot8 = lane8 >> 3

    def inner(s):
        y = s
        u = jnp.zeros_like(s)
        for h in range(5):
            y = y + xor_rows(y, 1 << h)
            u = u + w_low[h].reshape(4, 8, 128) * y
        t = y[0]
        top = jnp.zeros((8, 128), F32)
        for h in range(4):
            t = t + xor_lanes(t, slot8, 1 << h)
            top = top + w_top[h] * t
        return u + top[None]

    parts = [rho]
    sums = []
    for j in range(3):
        s = m[j]
        for k in range(j + 1):
            s = s + n[k] * parts[j - k]
        sums.append(s)
        parts.append(inner(s))
        rows_buf[j] = parts[j].reshape(32, 128)
    rows_buf[3] = parts[3].reshape(32, 128)

    def spread_of(c, u):
        return [sum(c[j] * u[j - k] for j in range(k, len(c))) for k in range(len(c))]

    def form(c, e, shift):
        whole = 0.0
        each = 0.0
        for j in range(len(c)):
            for k in range(j, len(c)):
                twice = 1.0 if j == k else 2.0
                t = j + k + shift
                whole = whole + (twice * c[j] * c[k]) * p[t]
                cross = c[j] * e[k] if j == k else c[j] * e[k] + c[k] * e[j]
                each = each + 2.0 * cross * m[t] + (twice * e[j]) * e[k] * n[t]
        return whole, each

    one = jnp.ones((8, 128), F32)
    d_c = [one]
    r_c = [one]
    x_c = [0.0, 0.0, 0.0]
    whole, each = form(d_c, [rho], 0)
    norm = whole + total(each)
    for it in range(3):
        d_e = spread_of(d_c, parts)
        image = sum(d_c[j] * parts[j + 1] for j in range(it + 1))
        whole, each = form(d_c, d_e, 1)
        curvature = whole + total(each + image * sum(d_c[j] * sums[j] for j in range(it + 1)))
        alpha = norm / curvature
        for k in range(it + 1):
            x_c[k] = x_c[k] + alpha * d_c[k]
        r_c = [a - alpha * i for a, i in zip(r_c + [0.0], [0.0] + d_c)]
        if it == 2:
            break
        whole, each = form(d_c, d_e, 2)
        along = sum(d_c[j] * m[j + 1] + d_e[j] * n[j + 1] for j in range(it + 1))
        square = whole + total(each + image * (2.0 * along + LEAF * image))
        after = alpha * alpha * square - norm
        beta = after / norm
        d_c = [a + beta * i for a, i in zip(r_c, d_c + [0.0])]
        norm = after

    mine = [rows_buf[k, pl.ds(b, 1), :] for k in range(4)]
    r_c = [c[0:1] for c in r_c]
    x_c = [c[0:1] for c in x_c]
    r_e = spread_of(r_c, mine)
    x_e = spread_of(x_c, mine)
    spare = jnp.zeros((1, 128), F32)
    values = r_e + x_e + [spare] + r_c[1:] + x_c + [spare, spare]
    back = jnp.concatenate([values[(16 - k) % 16] for k in range(16)], axis=0)
    send3[...] = turn_out(back).reshape(16, 1, 128)

    for offset in far_first((8, 2)):
        to = peer(g, offset, (8, 2))
        pltpu.make_async_remote_copy(
            src_ref=send3.at[lax.rem(16 - to, 16)], dst_ref=recv3.at[g], send_sem=ss3, recv_sem=rs3,
            device_id=(to, b), device_id_type=MESH,
        ).start()
    recv3[pl.ds(g, 1)] = send3[pl.ds(lax.rem(16 - g, 16), 1)]
    lift_r = jnp.zeros((128, 128), F32)
    lift_x = jnp.zeros((128, 128), F32)
    for k in range(4):
        lift_r = jnp.where(leaf_i == k, powers[k], lift_r)
        if k < 3:
            lift_x = jnp.where(leaf_i == 4 + k, powers[k], lift_x)
    lift = jnp.concatenate([lift_r.T[:, :16], lift_x.T[:, :16]], axis=0)
    pltpu.make_async_copy(recv3.at[pl.ds(0, GRP - 1)], recv3.at[pl.ds(0, GRP - 1)], rs3).wait()
    gains = turn_in(recv3[...].reshape(16, 128), g)
    gains = jnp.where((iota((16, 128), 1) & 7) == 7, 0.0, gains)
    lifted = exact_dot(lift, gains)
    r = lifted[:128] + v_buf[0]
    x = lifted[128:]
    for k in range(3):
        r = r + gains[8 + k : 9 + k] * v_buf[k + 1]
        x = x + gains[11 + k : 12 + k] * v_buf[k]
    x = x.T
    r = r.T
    for k in range(16):
        x_out[7 * k : 7 * k + 7, :] = x[8 * k : 8 * k + 7]
        r_out[7 * k : 7 * k + 7, :] = r[8 * k : 8 * k + 7]

    pltpu.make_async_copy(recv1.at[pl.ds(0, GRP - 1)], recv1.at[pl.ds(0, GRP - 1)], ss1).wait()
    pltpu.make_async_copy(recv2.at[pl.ds(0, 8 * (BASIN - 1))], recv2.at[pl.ds(0, 8 * (BASIN - 1))], ss2).wait()
    pltpu.make_async_copy(recv3.at[pl.ds(0, GRP - 1)], recv3.at[pl.ds(0, GRP - 1)], ss3).wait()


def hand_out(x, r, x_out, r_out, x_sem, r_sem):
    copies = [pltpu.make_async_copy(x, x_out, x_sem), pltpu.make_async_copy(r, r_out, r_sem)]
    for copy in copies:
        copy.start()
    for copy in copies:
        copy.wait()


def on_device(leaf_features, node_features, w_in, w_out, leaf_var, node_var, inner_var, sub_sizes):
    vmem = pl.BlockSpec(memory_space=pltpu.VMEM)
    hbm = pl.BlockSpec(memory_space=pltpu.HBM)
    tile = jax.ShapeDtypeStruct((112, 128), F32)
    x, r = pl.pallas_call(
        kernel,
        out_shape=(tile, tile),
        in_specs=[hbm] * 8,
        out_specs=(vmem, vmem),
        scratch_shapes=[
            pltpu.VMEM((16, 128, 128), BF16),
            pltpu.VMEM((11, 16, 128), BF16),
            pltpu.VMEM((512, 128), BF16),
            pltpu.VMEM((7, 512), BF16),
            pltpu.VMEM((1, 128), F32),
            pltpu.SMEM((1, 10), F32),
            pltpu.VMEM((1, 511), F32),
            pltpu.SMEM((1, 9), jnp.int32),
            pltpu.VMEM((4, 128, 128), F32),
            pltpu.VMEM((5, 32, 128), F32),
            pltpu.VMEM((4, 8, 128), F32),
            pltpu.VMEM((16, 1, 128), F32),
            pltpu.VMEM((16, 1, 128), F32),
            pltpu.VMEM((8, 128), F32),
            pltpu.VMEM((256, 128), F32),
            pltpu.VMEM((16, 1, 128), F32),
            pltpu.VMEM((16, 1, 128), F32),
            pltpu.VMEM((4, 32, 128), F32),
            pltpu.SemaphoreType.DMA((CHUNKS,)),
            pltpu.SemaphoreType.DMA((7,)),
        ]
        + [pltpu.SemaphoreType.DMA] * 6,
        compiler_params=pltpu.CompilerParams(collective_id=0, has_side_effects=True, vmem_limit_bytes=32 * 1024 * 1024),
    )(*[
        pltpu.with_memory_space_constraint(a, pltpu.HBM)
        for a in (
            leaf_features, jnp.transpose(node_features, (2, 0, 1)), w_in, w_out,
            leaf_var.reshape(1, -1), node_var.reshape(1, -1), inner_var.reshape(1, -1), sub_sizes,
        )
    ])

    here = pl.BlockSpec(memory_space=pl.ANY)
    return pl.pallas_call(
        hand_out,
        out_shape=(tile, tile),
        in_specs=[here] * 2,
        out_specs=(here, here),
        scratch_shapes=[pltpu.SemaphoreType.DMA, pltpu.SemaphoreType.DMA],
        compiler_params=pltpu.CompilerParams(vmem_limit_bytes=32 * 1024 * 1024),
    )(x, r)


def solution(mesh):
    return jax.shard_map(
        on_device,
        mesh=mesh,
        in_specs=(
            P(None, None, ("grp", "basin")),
            P(None, None, ("grp", "basin")),
            P(),
            P(),
            P(("grp", "basin")),
            P(("grp", "basin")),
            P(),
            P(("grp", "basin"), None),
        ),
        out_specs=(P(None, ("grp", "basin")), P(None, ("grp", "basin"))),
        check_vma=False,
    )
```

```python
import jax
import jax.numpy as jnp
from jax import lax
from jax.experimental import pallas as pl
from jax.experimental.pallas import tpu as pltpu
from jax.sharding import PartitionSpec as P

MESH = pl.DeviceIdType.MESH
F32 = jnp.float32
BF16 = jnp.bfloat16
LEAF = 128
GRP = 16
BASIN = 32
INNER = 7
CHUNKS = 2


def iota(shape, axis):
    return lax.broadcasted_iota(jnp.int32, shape, axis)


def far_first(sizes):
    a, b = sizes
    offsets = [(i, j) for i in range(a) for j in range(b) if i or j]
    return sorted(offsets, key=lambda o: -(min(o[0], a - o[0]) + min(o[1], b - o[1])))


def peer(index, offset, sizes):
    a, b = sizes
    shift = b.bit_length() - 1
    slow = ((index >> shift) + offset[0]) & (a - 1)
    return (slow << shift) + ((index + offset[1]) & (b - 1))


def turn_out(x):
    y = pltpu.roll(x, 0, 1, stride=8, stride_axis=0)
    slot = iota((16, 128), 1) >> 3
    for k in (1, 2, 4, 8):
        y = jnp.where((slot & k) != 0, pltpu.roll(y, 16 - k, 0), y)
    return y


def turn_in(x, me):
    y = pltpu.roll(x, 0, 1, stride=8, stride_axis=0)
    away = (iota((16, 128), 1) >> 3) - me
    for k in (1, 2, 4, 8):
        y = jnp.where((away & k) != 0, pltpu.roll(y, 16 - k, 0), y)
    y = pltpu.roll(y, 0, 1, stride=8, stride_axis=0)
    return pltpu.roll(y, lax.rem(128 - 8 * me, 128), 1)


def exact_dot(a, b):
    return jnp.dot(a, b, precision=lax.Precision.HIGHEST, preferred_element_type=F32)


def softplus(z):
    return jnp.maximum(z, 0.0) + jnp.log1p(jnp.exp(-jnp.abs(z)))


def pick(condition, value=1.0):
    return jnp.where(condition, value, 0.0).astype(F32)


def owner_of(index, height):
    return ((index >> height) << height) + (1 << (height - 1))


def xor_lanes(x, slot, bit):
    step = 8 * bit
    if step == 64:
        return pltpu.roll(x, 64, 1)
    return jnp.where((slot & bit) != 0, pltpu.roll(x, step, 1), pltpu.roll(x, 128 - step, 1))


def xor_rows(x, bit):
    if bit >= 8:
        far = bit // 8
        return jnp.concatenate([x[i ^ far : (i ^ far) + 1] for i in range(4)], axis=0)
    if bit == 4:
        return pltpu.roll(x, 4, 1)
    odd = (iota((4, 8, 128), 1) & bit) != 0
    return jnp.where(odd, pltpu.roll(x, bit, 1), pltpu.roll(x, 8 - bit, 1))


def total(x):
    y = (x[0] + x[1]) + (x[2] + x[3])
    for step in (4, 2, 1):
        y = y + pltpu.roll(y, step, 0)
    for step in (64, 32, 16, 8):
        y = y + pltpu.roll(y, step, 1)
    return y


def kernel(
    lf_in, nf_in, w_in_in, w_out_in, leaf_var_in, node_var_in, inner_var_in, sub_sizes_in,
    x_out, r_out,
    lf, nf, w_in, w_out, leaf_var, node_var, inner_var, sub_sizes, v_buf, w_low, w_top, send1, recv1, send2, recv2, send3, recv3, rows_buf,
    lf_sems, in_sems, ss1, rs1, ss2, rs2, ss3, rs3,
):
    g = lax.axis_index("grp")
    b = lax.axis_index("basin")
    q = g * BASIN + b
    each = 16 // CHUNKS
    pairs = (
        (w_in_in, w_in), (nf_in, nf), (w_out_in, w_out), (sub_sizes_in, sub_sizes),
        (node_var_in, node_var), (leaf_var_in, leaf_var), (inner_var_in, inner_var),
    )
    first = [pltpu.make_async_copy(a, c, in_sems.at[k]) for k, (a, c) in enumerate(pairs)]
    loads = [
        pltpu.make_async_copy(lf_in.at[pl.ds(each * c, each)], lf.at[pl.ds(each * c, each)], lf_sems.at[c])
        for c in range(CHUNKS)
    ]
    for load in first + loads:
        load.start()
    barrier = pltpu.get_barrier_semaphore()
    for step in range(1, GRP):
        pl.semaphore_signal(barrier, inc=1, device_id=(lax.rem(g + step, GRP), b), device_id_type=MESH)
    for step in range(1, BASIN):
        pl.semaphore_signal(barrier, inc=1, device_id=(g, lax.rem(b + step, BASIN)), device_id_type=MESH)

    for load in first + loads:
        load.wait()

    half = w_in[...] * jnp.asarray(0.5, BF16)
    eight = jnp.concatenate([w_out[...].astype(F32), jnp.zeros((1, 512), F32)], axis=0)
    out_all = jnp.concatenate([eight] * 16, axis=0).astype(BF16)

    def network(features):
        h = lax.dot_general(features, half, (((1,), (1,)), ((), ())), preferred_element_type=F32)
        hidden = (h + h * jnp.tanh(h)).astype(BF16)
        return lax.dot_general(hidden, out_all, (((1,), (1,)), ((), ())), preferred_element_type=F32)

    zn = network(nf[...].reshape(176, 128)).reshape(11, 16, 128)
    member3 = (iota((11, 16, 128), 2) >> 3) == iota((11, 16, 128), 1)
    zn = jnp.sum(jnp.where(member3, zn, 0.0), axis=1)
    soft_up = softplus(jnp.concatenate([zn, jnp.zeros((5, 128), F32)], axis=0))

    leaf_row = iota((1, 128), 1)
    leaf_i = iota((128, 128), 0)
    leaf_j = iota((128, 128), 1)
    label_row = jnp.zeros((1, 128), jnp.int32)
    label_i = jnp.zeros((128, 128), jnp.int32)
    end = jnp.int32(0)
    for s in range(9):
        end = end + sub_sizes[0, s]
        label_row = label_row + (leaf_row >= end).astype(jnp.int32)
        label_i = label_i + (leaf_i >= end).astype(jnp.int32)
    scale_row = jnp.zeros((1, 128), F32)
    one_row = jnp.ones((1, 128), F32)
    node16 = iota((16, 128), 0)
    node_inv = jnp.zeros((16, 128), F32)
    for s in range(9):
        var = node_var[0, s] * one_row
        scale_row = jnp.where(label_row == s, 1.0 / (sub_sizes[0, s].astype(F32) * var), scale_row)
        node_inv = jnp.where(node16 == s, 1.0 / var, node_inv)
    dev_var = node_var[0, 9] * one_row
    node_inv = jnp.where(node16 == 9, 1.0 / dev_var, node_inv)
    leaf_inv = 1.0 / leaf_var[...]
    op1 = (
        jnp.where(label_i == label_row, scale_row, 0.0)
        + 1.0 / (LEAF * dev_var)
        + jnp.where(leaf_i == leaf_j, leaf_inv, 0.0)
    )
    op2 = exact_dot(op1, op1)
    op3 = exact_dot(op2, op1)
    n1 = jnp.sum(op1, axis=0, keepdims=True)
    n2 = jnp.sum(op2, axis=0, keepdims=True)
    n3 = jnp.sum(op3, axis=0, keepdims=True)
    row8 = iota((8, 128), 0)
    low = jnp.where(row8 == 0, one_row, jnp.where(row8 == 1, n1, jnp.where(row8 == 2, n2, 0.0)))
    high = exact_dot(low, op3)
    n4 = high[1:2]
    n5 = high[2:3]
    powers = (one_row, n1, n2, n3, n4, n5)
    to_m = jnp.where(node16 == 0, one_row, 0.0)
    to_n = jnp.zeros((8, 128), F32)
    for k in range(1, 6):
        to_m = jnp.where(node16 == 16 - k, powers[k], to_m)
        to_n = jnp.where(row8 == k - 1, powers[k], to_n)
    lane8 = iota((8, 128), 1)
    n_col = jnp.sum(to_n, axis=1, keepdims=True)
    n_lanes = jnp.sum(jnp.where((lane8 & 7) == row8, n_col, 0.0), axis=0, keepdims=True)
    leaf_inv_col = jnp.sum(jnp.where(leaf_i == leaf_j, leaf_inv, 0.0), axis=1, keepdims=True)
    table = pick((leaf_j == label_i) | (leaf_j == 9))[:, :16]
    inner_row = inner_var[...]
    inner_at = iota((1, 511), 1)
    own_var = jnp.sum(jnp.where(inner_at == jnp.maximum(q - 1, 0), inner_row, 0.0), axis=1, keepdims=True)
    own_gain = jnp.where(q >= 1, 1.0 / own_var, 0.0)
    upper = exact_dot(table, soft_up * node_inv)

    lanes = leaf_j
    z = jnp.zeros((128, 128), F32)
    for c in range(CHUNKS):
        first_m = each * c
        some = network(jnp.concatenate([lf[first_m + k].T for k in range(each)], axis=0))
        for k in range(each):
            z = jnp.where((lanes >> 3) == first_m + k, some[128 * k : 128 * k + 128], z)
    b0 = softplus(z) * leaf_inv_col + upper
    applied = exact_dot(jnp.concatenate([op1, op2, op3, to_m], axis=0), b0)
    v1 = applied[:128]
    v2 = applied[128:256]
    v3 = applied[256:384]
    v_buf[0] = b0
    v_buf[1] = v1
    v_buf[2] = v2
    v_buf[3] = v3

    figures = applied[384:]
    figures = jnp.where(node16 == 10, n_lanes, figures)
    figures = jnp.where(node16 == 16 - INNER, soft_up[10:11] * own_gain, figures)
    products = (b0 * b0, b0 * v1, v1 * v1, v1 * v2, v2 * v2, v2 * v3)
    for k in range(6):
        figures = jnp.where(node16 == 8 - k, jnp.sum(products[k], axis=0, keepdims=True), figures)
    send1[...] = turn_out(figures).reshape(16, 1, 128)

    pl.semaphore_wait(barrier, GRP + BASIN - 2)

    for offset in far_first((8, 2)):
        to = peer(g, offset, (8, 2))
        pltpu.make_async_remote_copy(
            src_ref=send1.at[lax.rem(16 - to, 16)], dst_ref=recv1.at[g], send_sem=ss1, recv_sem=rs1,
            device_id=(to, b), device_id_type=MESH,
        ).start()
    recv1[pl.ds(g, 1)] = send1[pl.ds(lax.rem(16 - g, 16), 1)]

    at = iota((32, 511), 1) + 1
    spread = jnp.where((at & 31) == iota((32, 511), 0), inner_row, 0.0)
    at_col = iota((511, 128), 0) + 1
    to_slot = pick((at_col >> 5) == (iota((511, 128), 1) >> 3))
    var_of = exact_dot(spread, to_slot)
    low_row = iota((32, 32), 0)
    low_col = iota((32, 32), 1)
    row32 = iota((32, 128), 0)
    lane32 = iota((32, 128), 1)
    inverse = jnp.where((row32 == 0) & (lane32 < 8), 0.0, 1.0 / jnp.where((row32 == 0) & (lane32 < 8), 1.0, var_of))
    low_all = jnp.zeros((32, 32), F32)
    for h in range(1, 6):
        chosen = pick(low_col == owner_of(low_row, h))
        low_all = low_all + chosen
        w_low[h - 1] = exact_dot(chosen, inverse) * (1.0 / (LEAF * 2**h))
    from_lane = iota((128, 128), 0)
    top_all = jnp.zeros((128, 128), F32)
    same_day = (from_lane & 7) == (lanes & 7)
    for h in range(1, 5):
        chosen = pick(same_day & ((from_lane >> 3) == owner_of(lanes >> 3, h)))
        top_all = top_all + chosen
        w_top[h - 1] = exact_dot(jnp.broadcast_to(inverse[0:1], (8, 128)), chosen) * (1.0 / (LEAF * 2 ** (h + 5)))
    pad8 = (lane8 & 7) == 7
    to_pad = pick(((lanes & 7) == 7) & ((from_lane & 7) == (lanes >> 3)) & ((lanes >> 3) < 7))
    from_pad = pick(((from_lane & 7) == 7) & ((lanes & 7) == (from_lane >> 3)) & ((from_lane >> 3) < 7))
    same_slot = (from_lane >> 3) == (lanes >> 3)
    to_n_lanes = jnp.concatenate([pick(same_slot & ((from_lane & 7) == k)) for k in range(5)], axis=1)

    pltpu.make_async_copy(recv1.at[pl.ds(0, GRP - 1)], recv1.at[pl.ds(0, GRP - 1)], rs1).wait()
    turned = turn_in(recv1[...].reshape(16, 128), g)
    sums = exact_dot(turned[8:16], to_pad)
    send2[...] = jnp.where(pad8, sums, turned[:8])

    for offset in far_first((8, 4)):
        to = peer(b, offset, (8, 4))
        pltpu.make_async_remote_copy(
            src_ref=send2, dst_ref=recv2.at[pl.ds(pl.multiple_of(8 * b, 8), 8)], send_sem=ss2, recv_sem=rs2,
            device_id=(g, to), device_id_type=MESH,
        ).start()
    recv2[pl.ds(pl.multiple_of(8 * b, 8), 8), :] = send2[...]
    pltpu.make_async_copy(recv2.at[pl.ds(0, 8 * (BASIN - 1))], recv2.at[pl.ds(0, 8 * (BASIN - 1))], rs2).wait()

    everything = recv2[...].reshape(32, 8, 128)
    fluct = exact_dot(jnp.sum(everything, axis=0), from_pad)
    p = [jnp.broadcast_to(fluct[k : k + 1], (8, 128)) for k in range(6)]
    own = recv2[pl.ds(INNER, 32, stride=8), :]
    m = [recv2[pl.ds(k, 32, stride=8), :].reshape(4, 8, 128) for k in range(6)]
    n_all = exact_dot(recv2[pl.ds(6, 32, stride=8), :], to_n_lanes)
    n = [F32(LEAF)] + [n_all[:, 128 * k : 128 * k + 128].reshape(4, 8, 128) for k in range(5)]
    rho = exact_dot(low_all, own) + exact_dot(jnp.broadcast_to(own[0:1], (8, 128)), top_all)[0:1]
    rho = rho.reshape(4, 8, 128)
    slot8 = lane8 >> 3

    def inner(s):
        y = s
        u = jnp.zeros_like(s)
        for h in range(5):
            y = y + xor_rows(y, 1 << h)
            u = u + w_low[h].reshape(4, 8, 128) * y
        t = y[0]
        top = jnp.zeros((8, 128), F32)
        for h in range(4):
            t = t + xor_lanes(t, slot8, 1 << h)
            top = top + w_top[h] * t
        return u + top[None]

    parts = [rho]
    sums = []
    for j in range(3):
        s = m[j]
        for k in range(j + 1):
            s = s + n[k] * parts[j - k]
        sums.append(s)
        parts.append(inner(s))
        rows_buf[j] = parts[j].reshape(32, 128)
    rows_buf[3] = parts[3].reshape(32, 128)

    def spread_of(c, u):
        return [sum(c[j] * u[j - k] for j in range(k, len(c))) for k in range(len(c))]

    def form(c, e, shift):
        whole = 0.0
        each = 0.0
        for j in range(len(c)):
            for k in range(j, len(c)):
                twice = 1.0 if j == k else 2.0
                t = j + k + shift
                whole = whole + (twice * c[j] * c[k]) * p[t]
                cross = c[j] * e[k] if j == k else c[j] * e[k] + c[k] * e[j]
                each = each + 2.0 * cross * m[t] + (twice * e[j]) * e[k] * n[t]
        return whole, each

    one = jnp.ones((8, 128), F32)
    d_c = [one]
    r_c = [one]
    x_c = [0.0, 0.0, 0.0]
    whole, each = form(d_c, [rho], 0)
    norm = whole + total(each)
    for it in range(3):
        d_e = spread_of(d_c, parts)
        image = sum(d_c[j] * parts[j + 1] for j in range(it + 1))
        whole, each = form(d_c, d_e, 1)
        curvature = whole + total(each + image * sum(d_c[j] * sums[j] for j in range(it + 1)))
        alpha = norm / curvature
        for k in range(it + 1):
            x_c[k] = x_c[k] + alpha * d_c[k]
        r_c = [a - alpha * i for a, i in zip(r_c + [0.0], [0.0] + d_c)]
        if it == 2:
            break
        whole, each = form(d_c, d_e, 2)
        along = sum(d_c[j] * m[j + 1] + d_e[j] * n[j + 1] for j in range(it + 1))
        square = whole + total(each + image * (2.0 * along + LEAF * image))
        after = alpha * alpha * square - norm
        beta = after / norm
        d_c = [a + beta * i for a, i in zip(r_c, d_c + [0.0])]
        norm = after

    mine = [rows_buf[k, pl.ds(b, 1), :] for k in range(4)]
    r_c = [c[0:1] for c in r_c]
    x_c = [c[0:1] for c in x_c]
    r_e = spread_of(r_c, mine)
    x_e = spread_of(x_c, mine)
    spare = jnp.zeros((1, 128), F32)
    values = r_e + x_e + [spare] + r_c[1:] + x_c + [spare, spare]
    back = jnp.concatenate([values[(16 - k) % 16] for k in range(16)], axis=0)
    send3[...] = turn_out(back).reshape(16, 1, 128)

    for offset in far_first((8, 2)):
        to = peer(g, offset, (8, 2))
        pltpu.make_async_remote_copy(
            src_ref=send3.at[lax.rem(16 - to, 16)], dst_ref=recv3.at[g], send_sem=ss3, recv_sem=rs3,
            device_id=(to, b), device_id_type=MESH,
        ).start()
    recv3[pl.ds(g, 1)] = send3[pl.ds(lax.rem(16 - g, 16), 1)]
    lift_r = jnp.zeros((128, 128), F32)
    lift_x = jnp.zeros((128, 128), F32)
    for k in range(4):
        lift_r = jnp.where(leaf_i == k, powers[k], lift_r)
        if k < 3:
            lift_x = jnp.where(leaf_i == 4 + k, powers[k], lift_x)
    lift = jnp.concatenate([lift_r.T[:, :16], lift_x.T[:, :16]], axis=0)
    pltpu.make_async_copy(recv3.at[pl.ds(0, GRP - 1)], recv3.at[pl.ds(0, GRP - 1)], rs3).wait()
    gains = turn_in(recv3[...].reshape(16, 128), g)
    gains = jnp.where((iota((16, 128), 1) & 7) == 7, 0.0, gains)
    lifted = exact_dot(lift, gains)
    r = lifted[:128] + v_buf[0]
    x = lifted[128:]
    for k in range(3):
        r = r + gains[8 + k : 9 + k] * v_buf[k + 1]
        x = x + gains[11 + k : 12 + k] * v_buf[k]
    x = x.T
    r = r.T
    for k in range(16):
        x_out[7 * k : 7 * k + 7, :] = x[8 * k : 8 * k + 7]
        r_out[7 * k : 7 * k + 7, :] = r[8 * k : 8 * k + 7]

    pltpu.make_async_copy(recv1.at[pl.ds(0, GRP - 1)], recv1.at[pl.ds(0, GRP - 1)], ss1).wait()
    pltpu.make_async_copy(recv2.at[pl.ds(0, 8 * (BASIN - 1))], recv2.at[pl.ds(0, 8 * (BASIN - 1))], ss2).wait()
    pltpu.make_async_copy(recv3.at[pl.ds(0, GRP - 1)], recv3.at[pl.ds(0, GRP - 1)], ss3).wait()


def hand_out(x, r, x_out, r_out, x_sem, r_sem):
    copies = [pltpu.make_async_copy(x, x_out, x_sem), pltpu.make_async_copy(r, r_out, r_sem)]
    for copy in copies:
        copy.start()
    for copy in copies:
        copy.wait()


def on_device(leaf_features, node_features, w_in, w_out, leaf_var, node_var, inner_var, sub_sizes):
    vmem = pl.BlockSpec(memory_space=pltpu.VMEM)
    hbm = pl.BlockSpec(memory_space=pltpu.HBM)
    tile = jax.ShapeDtypeStruct((112, 128), F32)
    x, r = pl.pallas_call(
        kernel,
        out_shape=(tile, tile),
        in_specs=[hbm] * 8,
        out_specs=(vmem, vmem),
        scratch_shapes=[
            pltpu.VMEM((16, 128, 128), BF16),
            pltpu.VMEM((11, 16, 128), BF16),
            pltpu.VMEM((512, 128), BF16),
            pltpu.VMEM((7, 512), BF16),
            pltpu.VMEM((1, 128), F32),
            pltpu.SMEM((1, 10), F32),
            pltpu.VMEM((1, 511), F32),
            pltpu.SMEM((1, 9), jnp.int32),
            pltpu.VMEM((4, 128, 128), F32),
            pltpu.VMEM((5, 32, 128), F32),
            pltpu.VMEM((4, 8, 128), F32),
            pltpu.VMEM((16, 1, 128), F32),
            pltpu.VMEM((16, 1, 128), F32),
            pltpu.VMEM((8, 128), F32),
            pltpu.VMEM((256, 128), F32),
            pltpu.VMEM((16, 1, 128), F32),
            pltpu.VMEM((16, 1, 128), F32),
            pltpu.VMEM((4, 32, 128), F32),
            pltpu.SemaphoreType.DMA((CHUNKS,)),
            pltpu.SemaphoreType.DMA((7,)),
        ]
        + [pltpu.SemaphoreType.DMA] * 6,
        compiler_params=pltpu.CompilerParams(collective_id=0, has_side_effects=True, vmem_limit_bytes=32 * 1024 * 1024),
    )(*[
        pltpu.with_memory_space_constraint(a, pltpu.HBM)
        for a in (
            leaf_features, jnp.transpose(node_features, (2, 0, 1)), w_in, w_out,
            leaf_var.reshape(1, -1), node_var.reshape(1, -1), inner_var.reshape(1, -1), sub_sizes,
        )
    ])

    here = pl.BlockSpec(memory_space=pl.ANY)
    return pl.pallas_call(
        hand_out,
        out_shape=(tile, tile),
        in_specs=[here] * 2,
        out_specs=(here, here),
        scratch_shapes=[pltpu.SemaphoreType.DMA, pltpu.SemaphoreType.DMA],
        compiler_params=pltpu.CompilerParams(vmem_limit_bytes=32 * 1024 * 1024),
    )(x, r)


def solution(mesh):
    return jax.shard_map(
        on_device,
        mesh=mesh,
        in_specs=(
            P(None, None, ("grp", "basin")),
            P(None, None, ("grp", "basin")),
            P(),
            P(),
            P(("grp", "basin")),
            P(("grp", "basin")),
            P(),
            P(("grp", "basin"), None),
        ),
        out_specs=(P(None, ("grp", "basin")), P(None, ("grp", "basin"))),
        check_vma=False,
    )
```

```python
import jax
import jax.numpy as jnp
from jax import lax
from jax.experimental import pallas as pl
from jax.experimental.pallas import tpu as pltpu
from jax.sharding import PartitionSpec as P

MESH = pl.DeviceIdType.MESH
F32 = jnp.float32
BF16 = jnp.bfloat16
LEAF = 128
GRP = 16
BASIN = 32
INNER = 7
CHUNKS = 2


def iota(shape, axis):
    return lax.broadcasted_iota(jnp.int32, shape, axis)


def far_first(sizes):
    a, b = sizes
    offsets = [(i, j) for i in range(a) for j in range(b) if i or j]
    return sorted(offsets, key=lambda o: -(min(o[0], a - o[0]) + min(o[1], b - o[1])))


def peer(index, offset, sizes):
    a, b = sizes
    shift = b.bit_length() - 1
    slow = ((index >> shift) + offset[0]) & (a - 1)
    return (slow << shift) + ((index + offset[1]) & (b - 1))


def turn_out(x):
    y = pltpu.roll(x, 0, 1, stride=8, stride_axis=0)
    slot = iota((16, 128), 1) >> 3
    for k in (1, 2, 4, 8):
        y = jnp.where((slot & k) != 0, pltpu.roll(y, 16 - k, 0), y)
    return y


def turn_in(x, me):
    y = pltpu.roll(x, 0, 1, stride=8, stride_axis=0)
    away = (iota((16, 128), 1) >> 3) - me
    for k in (1, 2, 4, 8):
        y = jnp.where((away & k) != 0, pltpu.roll(y, 16 - k, 0), y)
    y = pltpu.roll(y, 0, 1, stride=8, stride_axis=0)
    return pltpu.roll(y, lax.rem(128 - 8 * me, 128), 1)


def exact_dot(a, b):
    return jnp.dot(a, b, precision=lax.Precision.HIGHEST, preferred_element_type=F32)


def softplus(z):
    return jnp.maximum(z, 0.0) + jnp.log1p(jnp.exp(-jnp.abs(z)))


def pick(condition, value=1.0):
    return jnp.where(condition, value, 0.0).astype(F32)


def owner_of(index, height):
    return ((index >> height) << height) + (1 << (height - 1))


def xor_lanes(x, slot, bit):
    step = 8 * bit
    if step == 64:
        return pltpu.roll(x, 64, 1)
    return jnp.where((slot & bit) != 0, pltpu.roll(x, step, 1), pltpu.roll(x, 128 - step, 1))


def xor_rows(x, bit):
    if bit >= 8:
        far = bit // 8
        return jnp.concatenate([x[i ^ far : (i ^ far) + 1] for i in range(4)], axis=0)
    if bit == 4:
        return pltpu.roll(x, 4, 1)
    odd = (iota((4, 8, 128), 1) & bit) != 0
    return jnp.where(odd, pltpu.roll(x, bit, 1), pltpu.roll(x, 8 - bit, 1))


def total(x):
    y = (x[0] + x[1]) + (x[2] + x[3])
    for step in (4, 2, 1):
        y = y + pltpu.roll(y, step, 0)
    for step in (64, 32, 16, 8):
        y = y + pltpu.roll(y, step, 1)
    return y


def kernel(
    lf_in, nf_in, w_in_in, w_out_in, leaf_var_in, node_var_in, inner_var_in, sub_sizes_in,
    x_out, r_out,
    lf, nf, w_in, w_out, leaf_var, node_var, inner_var, sub_sizes, v_buf, w_low, w_top, send1, recv1, send2, recv2, send3, recv3, rows_buf,
    lf_sems, in_sems, ss1, rs1, ss2, rs2, ss3, rs3,
):
    g = lax.axis_index("grp")
    b = lax.axis_index("basin")
    q = g * BASIN + b
    barrier = pltpu.get_barrier_semaphore()
    for step in range(1, BASIN):
        pl.semaphore_signal(barrier, inc=1, device_id=(g, lax.rem(b + step, BASIN)), device_id_type=MESH)
    for step in range(1, GRP):
        pl.semaphore_signal(barrier, inc=1, device_id=(lax.rem(g + step, GRP), b), device_id_type=MESH)
    each = 16 // CHUNKS
    pairs = (
        (w_in_in, w_in), (nf_in, nf), (w_out_in, w_out), (sub_sizes_in, sub_sizes),
        (node_var_in, node_var), (leaf_var_in, leaf_var), (inner_var_in, inner_var),
    )
    first = [pltpu.make_async_copy(a, c, in_sems.at[k]) for k, (a, c) in enumerate(pairs)]
    loads = [
        pltpu.make_async_copy(lf_in.at[pl.ds(each * c, each)], lf.at[pl.ds(each * c, each)], lf_sems.at[c])
        for c in range(CHUNKS)
    ]
    for load in first + loads:
        load.start()

    for load in first + loads:
        load.wait()

    half = w_in[...] * jnp.asarray(0.5, BF16)
    eight = jnp.concatenate([w_out[...].astype(F32), jnp.zeros((1, 512), F32)], axis=0)
    out_all = jnp.concatenate([eight] * 16, axis=0).astype(BF16)

    def network(features):
        h = lax.dot_general(features, half, (((1,), (1,)), ((), ())), preferred_element_type=F32)
        hidden = (h + h * jnp.tanh(h)).astype(BF16)
        return lax.dot_general(hidden, out_all, (((1,), (1,)), ((), ())), preferred_element_type=F32)

    zn = network(nf[...].reshape(176, 128)).reshape(11, 16, 128)
    member3 = (iota((11, 16, 128), 2) >> 3) == iota((11, 16, 128), 1)
    zn = jnp.sum(jnp.where(member3, zn, 0.0), axis=1)
    soft_up = softplus(jnp.concatenate([zn, jnp.zeros((5, 128), F32)], axis=0))

    leaf_row = iota((1, 128), 1)
    leaf_i = iota((128, 128), 0)
    leaf_j = iota((128, 128), 1)
    label_row = jnp.zeros((1, 128), jnp.int32)
    label_i = jnp.zeros((128, 128), jnp.int32)
    end = jnp.int32(0)
    for s in range(9):
        end = end + sub_sizes[0, s]
        label_row = label_row + (leaf_row >= end).astype(jnp.int32)
        label_i = label_i + (leaf_i >= end).astype(jnp.int32)
    scale_row = jnp.zeros((1, 128), F32)
    one_row = jnp.ones((1, 128), F32)
    node16 = iota((16, 128), 0)
    node_inv = jnp.zeros((16, 128), F32)
    for s in range(9):
        var = node_var[0, s] * one_row
        scale_row = jnp.where(label_row == s, 1.0 / (sub_sizes[0, s].astype(F32) * var), scale_row)
        node_inv = jnp.where(node16 == s, 1.0 / var, node_inv)
    dev_var = node_var[0, 9] * one_row
    node_inv = jnp.where(node16 == 9, 1.0 / dev_var, node_inv)
    leaf_inv = 1.0 / leaf_var[...]
    op1 = (
        jnp.where(label_i == label_row, scale_row, 0.0)
        + 1.0 / (LEAF * dev_var)
        + jnp.where(leaf_i == leaf_j, leaf_inv, 0.0)
    )
    op2 = exact_dot(op1, op1)
    op3 = exact_dot(op2, op1)
    n1 = jnp.sum(op1, axis=0, keepdims=True)
    n2 = jnp.sum(op2, axis=0, keepdims=True)
    n3 = jnp.sum(op3, axis=0, keepdims=True)
    row8 = iota((8, 128), 0)
    low = jnp.where(row8 == 0, one_row, jnp.where(row8 == 1, n1, jnp.where(row8 == 2, n2, 0.0)))
    high = exact_dot(low, op3)
    n4 = high[1:2]
    n5 = high[2:3]
    powers = (one_row, n1, n2, n3, n4, n5)
    to_m = jnp.where(node16 == 0, one_row, 0.0)
    to_n = jnp.zeros((8, 128), F32)
    for k in range(1, 6):
        to_m = jnp.where(node16 == 16 - k, powers[k], to_m)
        to_n = jnp.where(row8 == k - 1, powers[k], to_n)
    lane8 = iota((8, 128), 1)
    n_col = jnp.sum(to_n, axis=1, keepdims=True)
    n_lanes = jnp.sum(jnp.where((lane8 & 7) == row8, n_col, 0.0), axis=0, keepdims=True)
    leaf_inv_col = jnp.sum(jnp.where(leaf_i == leaf_j, leaf_inv, 0.0), axis=1, keepdims=True)
    table = pick((leaf_j == label_i) | (leaf_j == 9))[:, :16]
    inner_row = inner_var[...]
    inner_at = iota((1, 511), 1)
    own_var = jnp.sum(jnp.where(inner_at == jnp.maximum(q - 1, 0), inner_row, 0.0), axis=1, keepdims=True)
    own_gain = jnp.where(q >= 1, 1.0 / own_var, 0.0)
    upper = exact_dot(table, soft_up * node_inv)

    lanes = leaf_j
    z = jnp.zeros((128, 128), F32)
    for c in range(CHUNKS):
        first_m = each * c
        some = network(jnp.concatenate([lf[first_m + k].T for k in range(each)], axis=0))
        for k in range(each):
            z = jnp.where((lanes >> 3) == first_m + k, some[128 * k : 128 * k + 128], z)
    b0 = softplus(z) * leaf_inv_col + upper
    applied = exact_dot(jnp.concatenate([op1, op2, op3, to_m], axis=0), b0)
    v1 = applied[:128]
    v2 = applied[128:256]
    v3 = applied[256:384]
    v_buf[0] = b0
    v_buf[1] = v1
    v_buf[2] = v2
    v_buf[3] = v3

    figures = applied[384:]
    figures = jnp.where(node16 == 10, n_lanes, figures)
    figures = jnp.where(node16 == 16 - INNER, soft_up[10:11] * own_gain, figures)
    products = (b0 * b0, b0 * v1, v1 * v1, v1 * v2, v2 * v2, v2 * v3)
    for k in range(6):
        figures = jnp.where(node16 == 8 - k, jnp.sum(products[k], axis=0, keepdims=True), figures)
    send1[...] = turn_out(figures).reshape(16, 1, 128)

    pl.semaphore_wait(barrier, GRP + BASIN - 2)

    for offset in far_first((8, 2)):
        to = peer(g, offset, (8, 2))
        pltpu.make_async_remote_copy(
            src_ref=send1.at[lax.rem(16 - to, 16)], dst_ref=recv1.at[g], send_sem=ss1, recv_sem=rs1,
            device_id=(to, b), device_id_type=MESH,
        ).start()
    recv1[pl.ds(g, 1)] = send1[pl.ds(lax.rem(16 - g, 16), 1)]

    at = iota((32, 511), 1) + 1
    spread = jnp.where((at & 31) == iota((32, 511), 0), inner_row, 0.0)
    at_col = iota((511, 128), 0) + 1
    to_slot = pick((at_col >> 5) == (iota((511, 128), 1) >> 3))
    var_of = exact_dot(spread, to_slot)
    low_row = iota((32, 32), 0)
    low_col = iota((32, 32), 1)
    row32 = iota((32, 128), 0)
    lane32 = iota((32, 128), 1)
    inverse = jnp.where((row32 == 0) & (lane32 < 8), 0.0, 1.0 / jnp.where((row32 == 0) & (lane32 < 8), 1.0, var_of))
    low_all = jnp.zeros((32, 32), F32)
    for h in range(1, 6):
        chosen = pick(low_col == owner_of(low_row, h))
        low_all = low_all + chosen
        w_low[h - 1] = exact_dot(chosen, inverse) * (1.0 / (LEAF * 2**h))
    from_lane = iota((128, 128), 0)
    top_all = jnp.zeros((128, 128), F32)
    same_day = (from_lane & 7) == (lanes & 7)
    for h in range(1, 5):
        chosen = pick(same_day & ((from_lane >> 3) == owner_of(lanes >> 3, h)))
        top_all = top_all + chosen
        w_top[h - 1] = exact_dot(jnp.broadcast_to(inverse[0:1], (8, 128)), chosen) * (1.0 / (LEAF * 2 ** (h + 5)))
    pad8 = (lane8 & 7) == 7
    to_pad = pick(((lanes & 7) == 7) & ((from_lane & 7) == (lanes >> 3)) & ((lanes >> 3) < 7))
    from_pad = pick(((from_lane & 7) == 7) & ((lanes & 7) == (from_lane >> 3)) & ((from_lane >> 3) < 7))
    same_slot = (from_lane >> 3) == (lanes >> 3)
    to_n_lanes = jnp.concatenate([pick(same_slot & ((from_lane & 7) == k)) for k in range(5)], axis=1)

    pltpu.make_async_copy(recv1.at[pl.ds(0, GRP - 1)], recv1.at[pl.ds(0, GRP - 1)], rs1).wait()
    turned = turn_in(recv1[...].reshape(16, 128), g)
    sums = exact_dot(turned[8:16], to_pad)
    send2[...] = jnp.where(pad8, sums, turned[:8])

    for offset in far_first((8, 4)):
        to = peer(b, offset, (8, 4))
        pltpu.make_async_remote_copy(
            src_ref=send2, dst_ref=recv2.at[pl.ds(pl.multiple_of(8 * b, 8), 8)], send_sem=ss2, recv_sem=rs2,
            device_id=(g, to), device_id_type=MESH,
        ).start()
    recv2[pl.ds(pl.multiple_of(8 * b, 8), 8), :] = send2[...]
    pltpu.make_async_copy(recv2.at[pl.ds(0, 8 * (BASIN - 1))], recv2.at[pl.ds(0, 8 * (BASIN - 1))], rs2).wait()

    everything = recv2[...].reshape(32, 8, 128)
    fluct = exact_dot(jnp.sum(everything, axis=0), from_pad)
    p = [jnp.broadcast_to(fluct[k : k + 1], (8, 128)) for k in range(6)]
    own = recv2[pl.ds(INNER, 32, stride=8), :]
    m = [recv2[pl.ds(k, 32, stride=8), :].reshape(4, 8, 128) for k in range(6)]
    n_all = exact_dot(recv2[pl.ds(6, 32, stride=8), :], to_n_lanes)
    n = [F32(LEAF)] + [n_all[:, 128 * k : 128 * k + 128].reshape(4, 8, 128) for k in range(5)]
    rho = exact_dot(low_all, own) + exact_dot(jnp.broadcast_to(own[0:1], (8, 128)), top_all)[0:1]
    rho = rho.reshape(4, 8, 128)
    slot8 = lane8 >> 3

    def inner(s):
        y = s
        u = jnp.zeros_like(s)
        for h in range(5):
            y = y + xor_rows(y, 1 << h)
            u = u + w_low[h].reshape(4, 8, 128) * y
        t = y[0]
        top = jnp.zeros((8, 128), F32)
        for h in range(4):
            t = t + xor_lanes(t, slot8, 1 << h)
            top = top + w_top[h] * t
        return u + top[None]

    parts = [rho]
    sums = []
    for j in range(3):
        s = m[j]
        for k in range(j + 1):
            s = s + n[k] * parts[j - k]
        sums.append(s)
        parts.append(inner(s))
        rows_buf[j] = parts[j].reshape(32, 128)
    rows_buf[3] = parts[3].reshape(32, 128)

    def spread_of(c, u):
        return [sum(c[j] * u[j - k] for j in range(k, len(c))) for k in range(len(c))]

    def form(c, e, shift):
        whole = 0.0
        each = 0.0
        for j in range(len(c)):
            for k in range(j, len(c)):
                twice = 1.0 if j == k else 2.0
                t = j + k + shift
                whole = whole + (twice * c[j] * c[k]) * p[t]
                cross = c[j] * e[k] if j == k else c[j] * e[k] + c[k] * e[j]
                each = each + 2.0 * cross * m[t] + (twice * e[j]) * e[k] * n[t]
        return whole, each

    one = jnp.ones((8, 128), F32)
    d_c = [one]
    r_c = [one]
    x_c = [0.0, 0.0, 0.0]
    whole, each = form(d_c, [rho], 0)
    norm = whole + total(each)
    for it in range(3):
        d_e = spread_of(d_c, parts)
        image = sum(d_c[j] * parts[j + 1] for j in range(it + 1))
        whole, each = form(d_c, d_e, 1)
        curvature = whole + total(each + image * sum(d_c[j] * sums[j] for j in range(it + 1)))
        alpha = norm / curvature
        for k in range(it + 1):
            x_c[k] = x_c[k] + alpha * d_c[k]
        r_c = [a - alpha * i for a, i in zip(r_c + [0.0], [0.0] + d_c)]
        if it == 2:
            break
        whole, each = form(d_c, d_e, 2)
        along = sum(d_c[j] * m[j + 1] + d_e[j] * n[j + 1] for j in range(it + 1))
        square = whole + total(each + image * (2.0 * along + LEAF * image))
        after = alpha * alpha * square - norm
        beta = after / norm
        d_c = [a + beta * i for a, i in zip(r_c, d_c + [0.0])]
        norm = after

    mine = [rows_buf[k, pl.ds(b, 1), :] for k in range(4)]
    r_c = [c[0:1] for c in r_c]
    x_c = [c[0:1] for c in x_c]
    r_e = spread_of(r_c, mine)
    x_e = spread_of(x_c, mine)
    spare = jnp.zeros((1, 128), F32)
    values = r_e + x_e + [spare] + r_c[1:] + x_c + [spare, spare]
    back = jnp.concatenate([values[(16 - k) % 16] for k in range(16)], axis=0)
    send3[...] = turn_out(back).reshape(16, 1, 128)

    for offset in far_first((8, 2)):
        to = peer(g, offset, (8, 2))
        pltpu.make_async_remote_copy(
            src_ref=send3.at[lax.rem(16 - to, 16)], dst_ref=recv3.at[g], send_sem=ss3, recv_sem=rs3,
            device_id=(to, b), device_id_type=MESH,
        ).start()
    recv3[pl.ds(g, 1)] = send3[pl.ds(lax.rem(16 - g, 16), 1)]
    lift_r = jnp.zeros((128, 128), F32)
    lift_x = jnp.zeros((128, 128), F32)
    for k in range(4):
        lift_r = jnp.where(leaf_i == k, powers[k], lift_r)
        if k < 3:
            lift_x = jnp.where(leaf_i == 4 + k, powers[k], lift_x)
    lift = jnp.concatenate([lift_r.T[:, :16], lift_x.T[:, :16]], axis=0)
    pltpu.make_async_copy(recv3.at[pl.ds(0, GRP - 1)], recv3.at[pl.ds(0, GRP - 1)], rs3).wait()
    gains = turn_in(recv3[...].reshape(16, 128), g)
    gains = jnp.where((iota((16, 128), 1) & 7) == 7, 0.0, gains)
    lifted = exact_dot(lift, gains)
    r = lifted[:128] + v_buf[0]
    x = lifted[128:]
    for k in range(3):
        r = r + gains[8 + k : 9 + k] * v_buf[k + 1]
        x = x + gains[11 + k : 12 + k] * v_buf[k]
    x = x.T
    r = r.T
    for k in range(16):
        x_out[7 * k : 7 * k + 7, :] = x[8 * k : 8 * k + 7]
        r_out[7 * k : 7 * k + 7, :] = r[8 * k : 8 * k + 7]

    pltpu.make_async_copy(recv1.at[pl.ds(0, GRP - 1)], recv1.at[pl.ds(0, GRP - 1)], ss1).wait()
    pltpu.make_async_copy(recv2.at[pl.ds(0, 8 * (BASIN - 1))], recv2.at[pl.ds(0, 8 * (BASIN - 1))], ss2).wait()
    pltpu.make_async_copy(recv3.at[pl.ds(0, GRP - 1)], recv3.at[pl.ds(0, GRP - 1)], ss3).wait()


def hand_out(x, r, x_out, r_out, x_sem, r_sem):
    copies = [pltpu.make_async_copy(x, x_out, x_sem), pltpu.make_async_copy(r, r_out, r_sem)]
    for copy in copies:
        copy.start()
    for copy in copies:
        copy.wait()


def on_device(leaf_features, node_features, w_in, w_out, leaf_var, node_var, inner_var, sub_sizes):
    vmem = pl.BlockSpec(memory_space=pltpu.VMEM)
    hbm = pl.BlockSpec(memory_space=pltpu.HBM)
    tile = jax.ShapeDtypeStruct((112, 128), F32)
    x, r = pl.pallas_call(
        kernel,
        out_shape=(tile, tile),
        in_specs=[hbm] * 8,
        out_specs=(vmem, vmem),
        scratch_shapes=[
            pltpu.VMEM((16, 128, 128), BF16),
            pltpu.VMEM((11, 16, 128), BF16),
            pltpu.VMEM((512, 128), BF16),
            pltpu.VMEM((7, 512), BF16),
            pltpu.VMEM((1, 128), F32),
            pltpu.SMEM((1, 10), F32),
            pltpu.VMEM((1, 511), F32),
            pltpu.SMEM((1, 9), jnp.int32),
            pltpu.VMEM((4, 128, 128), F32),
            pltpu.VMEM((5, 32, 128), F32),
            pltpu.VMEM((4, 8, 128), F32),
            pltpu.VMEM((16, 1, 128), F32),
            pltpu.VMEM((16, 1, 128), F32),
            pltpu.VMEM((8, 128), F32),
            pltpu.VMEM((256, 128), F32),
            pltpu.VMEM((16, 1, 128), F32),
            pltpu.VMEM((16, 1, 128), F32),
            pltpu.VMEM((4, 32, 128), F32),
            pltpu.SemaphoreType.DMA((CHUNKS,)),
            pltpu.SemaphoreType.DMA((7,)),
        ]
        + [pltpu.SemaphoreType.DMA] * 6,
        compiler_params=pltpu.CompilerParams(collective_id=0, has_side_effects=True, vmem_limit_bytes=32 * 1024 * 1024),
    )(*[
        pltpu.with_memory_space_constraint(a, pltpu.HBM)
        for a in (
            leaf_features, jnp.transpose(node_features, (2, 0, 1)), w_in, w_out,
            leaf_var.reshape(1, -1), node_var.reshape(1, -1), inner_var.reshape(1, -1), sub_sizes,
        )
    ])

    here = pl.BlockSpec(memory_space=pl.ANY)
    return pl.pallas_call(
        hand_out,
        out_shape=(tile, tile),
        in_specs=[here] * 2,
        out_specs=(here, here),
        scratch_shapes=[pltpu.SemaphoreType.DMA, pltpu.SemaphoreType.DMA],
        compiler_params=pltpu.CompilerParams(vmem_limit_bytes=32 * 1024 * 1024),
    )(x, r)


def solution(mesh):
    return jax.shard_map(
        on_device,
        mesh=mesh,
        in_specs=(
            P(None, None, ("grp", "basin")),
            P(None, None, ("grp", "basin")),
            P(),
            P(),
            P(("grp", "basin")),
            P(("grp", "basin")),
            P(),
            P(("grp", "basin"), None),
        ),
        out_specs=(P(None, ("grp", "basin")), P(None, ("grp", "basin"))),
        check_vma=False,
    )
```

```python
import jax
import jax.numpy as jnp
from jax import lax
from jax.experimental import pallas as pl
from jax.experimental.pallas import tpu as pltpu
from jax.sharding import PartitionSpec as P

MESH = pl.DeviceIdType.MESH
F32 = jnp.float32
BF16 = jnp.bfloat16
LEAF = 128
GRP = 16
BASIN = 32
INNER = 7
CHUNKS = 2


def iota(shape, axis):
    return lax.broadcasted_iota(jnp.int32, shape, axis)


def far_first(sizes):
    a, b = sizes
    offsets = [(i, j) for i in range(a) for j in range(b) if i or j]
    return sorted(offsets, key=lambda o: -(min(o[0], a - o[0]) + min(o[1], b - o[1])))


def peer(index, offset, sizes):
    a, b = sizes
    shift = b.bit_length() - 1
    slow = ((index >> shift) + offset[0]) & (a - 1)
    return (slow << shift) + ((index + offset[1]) & (b - 1))


def turn_out(x):
    y = pltpu.roll(x, 0, 1, stride=8, stride_axis=0)
    slot = iota((16, 128), 1) >> 3
    for k in (1, 2, 4, 8):
        y = jnp.where((slot & k) != 0, pltpu.roll(y, 16 - k, 0), y)
    return y


def turn_in(x, me):
    y = pltpu.roll(x, 0, 1, stride=8, stride_axis=0)
    away = (iota((16, 128), 1) >> 3) - me
    for k in (1, 2, 4, 8):
        y = jnp.where((away & k) != 0, pltpu.roll(y, 16 - k, 0), y)
    y = pltpu.roll(y, 0, 1, stride=8, stride_axis=0)
    return pltpu.roll(y, lax.rem(128 - 8 * me, 128), 1)


def exact_dot(a, b):
    return jnp.dot(a, b, precision=lax.Precision.HIGHEST, preferred_element_type=F32)


def softplus(z):
    return jnp.maximum(z, 0.0) + jnp.log1p(jnp.exp(-jnp.abs(z)))


def pick(condition, value=1.0):
    return jnp.where(condition, value, 0.0).astype(F32)


def owner_of(index, height):
    return ((index >> height) << height) + (1 << (height - 1))


def xor_lanes(x, slot, bit):
    step = 8 * bit
    if step == 64:
        return pltpu.roll(x, 64, 1)
    return jnp.where((slot & bit) != 0, pltpu.roll(x, step, 1), pltpu.roll(x, 128 - step, 1))


def xor_rows(x, bit):
    if bit >= 8:
        far = bit // 8
        return jnp.concatenate([x[i ^ far : (i ^ far) + 1] for i in range(4)], axis=0)
    if bit == 4:
        return pltpu.roll(x, 4, 1)
    odd = (iota((4, 8, 128), 1) & bit) != 0
    return jnp.where(odd, pltpu.roll(x, bit, 1), pltpu.roll(x, 8 - bit, 1))


def total(x):
    y = (x[0] + x[1]) + (x[2] + x[3])
    for step in (4, 2, 1):
        y = y + pltpu.roll(y, step, 0)
    for step in (64, 32, 16, 8):
        y = y + pltpu.roll(y, step, 1)
    return y


def kernel(
    lf_in, nf_in, w_in_in, w_out_in, leaf_var_in, node_var_in, inner_var_in, sub_sizes_in,
    x_out, r_out,
    lf, nf, w_in, w_out, leaf_var, node_var, inner_var, sub_sizes, v_buf, w_low, w_top, send1, recv1, send2, recv2, send3, recv3, rows_buf,
    lf_sems, in_sems, ss1, rs1, ss2, rs2, ss3, rs3,
):
    g = lax.axis_index("grp")
    b = lax.axis_index("basin")
    q = g * BASIN + b
    each = 16 // CHUNKS
    pairs = (
        (w_in_in, w_in), (nf_in, nf), (w_out_in, w_out), (sub_sizes_in, sub_sizes),
        (node_var_in, node_var), (leaf_var_in, leaf_var), (inner_var_in, inner_var),
    )
    first = [pltpu.make_async_copy(a, c, in_sems.at[k]) for k, (a, c) in enumerate(pairs)]
    loads = [
        pltpu.make_async_copy(lf_in.at[pl.ds(each * c, each)], lf.at[pl.ds(each * c, each)], lf_sems.at[c])
        for c in range(CHUNKS)
    ]
    for load in first + loads:
        load.start()
    barrier = pltpu.get_barrier_semaphore()
    for step in range(1, GRP):
        pl.semaphore_signal(barrier, inc=1, device_id=(lax.rem(g + step, GRP), b), device_id_type=MESH)
    for step in range(1, BASIN):
        pl.semaphore_signal(barrier, inc=1, device_id=(g, lax.rem(b + step, BASIN)), device_id_type=MESH)

    for load in first:
        load.wait()

    half = w_in[...] * jnp.asarray(0.5, BF16)
    eight = jnp.concatenate([w_out[...].astype(F32), jnp.zeros((1, 512), F32)], axis=0)
    out_all = jnp.concatenate([eight] * 16, axis=0).astype(BF16)

    def network(features):
        h = lax.dot_general(features, half, (((1,), (1,)), ((), ())), preferred_element_type=F32)
        hidden = (h + h * jnp.tanh(h)).astype(BF16)
        return lax.dot_general(hidden, out_all, (((1,), (1,)), ((), ())), preferred_element_type=F32)

    zn = network(nf[...].reshape(176, 128)).reshape(11, 16, 128)
    member3 = (iota((11, 16, 128), 2) >> 3) == iota((11, 16, 128), 1)
    zn = jnp.sum(jnp.where(member3, zn, 0.0), axis=1)
    soft_up = softplus(jnp.concatenate([zn, jnp.zeros((5, 128), F32)], axis=0))

    leaf_row = iota((1, 128), 1)
    leaf_i = iota((128, 128), 0)
    leaf_j = iota((128, 128), 1)
    label_row = jnp.zeros((1, 128), jnp.int32)
    label_i = jnp.zeros((128, 128), jnp.int32)
    end = jnp.int32(0)
    for s in range(9):
        end = end + sub_sizes[0, s]
        label_row = label_row + (leaf_row >= end).astype(jnp.int32)
        label_i = label_i + (leaf_i >= end).astype(jnp.int32)
    scale_row = jnp.zeros((1, 128), F32)
    one_row = jnp.ones((1, 128), F32)
    node16 = iota((16, 128), 0)
    node_inv = jnp.zeros((16, 128), F32)
    for s in range(9):
        var = node_var[0, s] * one_row
        scale_row = jnp.where(label_row == s, 1.0 / (sub_sizes[0, s].astype(F32) * var), scale_row)
        node_inv = jnp.where(node16 == s, 1.0 / var, node_inv)
    dev_var = node_var[0, 9] * one_row
    node_inv = jnp.where(node16 == 9, 1.0 / dev_var, node_inv)
    leaf_inv = 1.0 / leaf_var[...]
    op1 = (
        jnp.where(label_i == label_row, scale_row, 0.0)
        + 1.0 / (LEAF * dev_var)
        + jnp.where(leaf_i == leaf_j, leaf_inv, 0.0)
    )
    op2 = exact_dot(op1, op1)
    op3 = exact_dot(op2, op1)
    n1 = jnp.sum(op1, axis=0, keepdims=True)
    n2 = jnp.sum(op2, axis=0, keepdims=True)
    n3 = jnp.sum(op3, axis=0, keepdims=True)
    row8 = iota((8, 128), 0)
    low = jnp.where(row8 == 0, one_row, jnp.where(row8 == 1, n1, jnp.where(row8 == 2, n2, 0.0)))
    high = exact_dot(low, op3)
    n4 = high[1:2]
    n5 = high[2:3]
    powers = (one_row, n1, n2, n3, n4, n5)
    to_m = jnp.where(node16 == 0, one_row, 0.0)
    to_n = jnp.zeros((8, 128), F32)
    for k in range(1, 6):
        to_m = jnp.where(node16 == 16 - k, powers[k], to_m)
        to_n = jnp.where(row8 == k - 1, powers[k], to_n)
    lane8 = iota((8, 128), 1)
    n_col = jnp.sum(to_n, axis=1, keepdims=True)
    n_lanes = jnp.sum(jnp.where((lane8 & 7) == row8, n_col, 0.0), axis=0, keepdims=True)
    leaf_inv_col = jnp.sum(jnp.where(leaf_i == leaf_j, leaf_inv, 0.0), axis=1, keepdims=True)
    table = pick((leaf_j == label_i) | (leaf_j == 9))[:, :16]
    inner_row = inner_var[...]
    inner_at = iota((1, 511), 1)
    own_var = jnp.sum(jnp.where(inner_at == jnp.maximum(q - 1, 0), inner_row, 0.0), axis=1, keepdims=True)
    own_gain = jnp.where(q >= 1, 1.0 / own_var, 0.0)
    upper = exact_dot(table, soft_up * node_inv)

    lanes = leaf_j
    z = jnp.zeros((128, 128), F32)
    for c in range(CHUNKS):
        loads[c].wait()
        first_m = each * c
        some = network(jnp.concatenate([lf[first_m + k].T for k in range(each)], axis=0))
        for k in range(each):
            z = jnp.where((lanes >> 3) == first_m + k, some[128 * k : 128 * k + 128], z)
    b0 = softplus(z) * leaf_inv_col + upper
    applied = exact_dot(jnp.concatenate([op1, op2, op3, to_m], axis=0), b0)
    v1 = applied[:128]
    v2 = applied[128:256]
    v3 = applied[256:384]
    v_buf[0] = b0
    v_buf[1] = v1
    v_buf[2] = v2
    v_buf[3] = v3

    figures = applied[384:]
    figures = jnp.where(node16 == 10, n_lanes, figures)
    figures = jnp.where(node16 == 16 - INNER, soft_up[10:11] * own_gain, figures)
    products = (b0 * b0, b0 * v1, v1 * v1, v1 * v2, v2 * v2, v2 * v3)
    for k in range(6):
        figures = jnp.where(node16 == 8 - k, jnp.sum(products[k], axis=0, keepdims=True), figures)
    send1[...] = turn_out(figures).reshape(16, 1, 128)

    pl.semaphore_wait(barrier, GRP + BASIN - 2)

    for offset in far_first((8, 2)):
        to = peer(g, offset, (8, 2))
        pltpu.make_async_remote_copy(
            src_ref=send1.at[lax.rem(16 - to, 16)], dst_ref=recv1.at[g], send_sem=ss1, recv_sem=rs1,
            device_id=(to, b), device_id_type=MESH,
        ).start()
    recv1[pl.ds(g, 1)] = send1[pl.ds(lax.rem(16 - g, 16), 1)]

    at = iota((32, 511), 1) + 1
    spread = jnp.where((at & 31) == iota((32, 511), 0), inner_row, 0.0)
    at_col = iota((511, 128), 0) + 1
    to_slot = pick((at_col >> 5) == (iota((511, 128), 1) >> 3))
    var_of = exact_dot(spread, to_slot)
    low_row = iota((32, 32), 0)
    low_col = iota((32, 32), 1)
    row32 = iota((32, 128), 0)
    lane32 = iota((32, 128), 1)
    inverse = jnp.where((row32 == 0) & (lane32 < 8), 0.0, 1.0 / jnp.where((row32 == 0) & (lane32 < 8), 1.0, var_of))
    low_all = jnp.zeros((32, 32), F32)
    for h in range(1, 6):
        chosen = pick(low_col == owner_of(low_row, h))
        low_all = low_all + chosen
        w_low[h - 1] = exact_dot(chosen, inverse) * (1.0 / (LEAF * 2**h))
    from_lane = iota((128, 128), 0)
    top_all = jnp.zeros((128, 128), F32)
    same_day = (from_lane & 7) == (lanes & 7)
    for h in range(1, 5):
        chosen = pick(same_day & ((from_lane >> 3) == owner_of(lanes >> 3, h)))
        top_all = top_all + chosen
        w_top[h - 1] = exact_dot(jnp.broadcast_to(inverse[0:1], (8, 128)), chosen) * (1.0 / (LEAF * 2 ** (h + 5)))
    pad8 = (lane8 & 7) == 7
    to_pad = pick(((lanes & 7) == 7) & ((from_lane & 7) == (lanes >> 3)) & ((lanes >> 3) < 7))
    from_pad = pick(((from_lane & 7) == 7) & ((lanes & 7) == (from_lane >> 3)) & ((from_lane >> 3) < 7))
    same_slot = (from_lane >> 3) == (lanes >> 3)
    to_n_lanes = jnp.concatenate([pick(same_slot & ((from_lane & 7) == k)) for k in range(5)], axis=1)

    pltpu.make_async_copy(recv1.at[pl.ds(0, GRP - 1)], recv1.at[pl.ds(0, GRP - 1)], rs1).wait()
    turned = turn_in(recv1[...].reshape(16, 128), g)
    sums = exact_dot(turned[8:16], to_pad)
    send2[...] = jnp.where(pad8, sums, turned[:8])

    for offset in far_first((8, 4)):
        to = peer(b, offset, (8, 4))
        pltpu.make_async_remote_copy(
            src_ref=send2, dst_ref=recv2.at[pl.ds(pl.multiple_of(8 * b, 8), 8)], send_sem=ss2, recv_sem=rs2,
            device_id=(g, to), device_id_type=MESH,
        ).start()
    recv2[pl.ds(pl.multiple_of(8 * b, 8), 8), :] = send2[...]
    pltpu.make_async_copy(recv2.at[pl.ds(0, 8 * (BASIN - 1))], recv2.at[pl.ds(0, 8 * (BASIN - 1))], rs2).wait()

    everything = recv2[...].reshape(32, 8, 128)
    fluct = exact_dot(jnp.sum(everything, axis=0), from_pad)
    p = [jnp.broadcast_to(fluct[k : k + 1], (8, 128)) for k in range(6)]
    own = recv2[pl.ds(INNER, 32, stride=8), :]
    m = [recv2[pl.ds(k, 32, stride=8), :].reshape(4, 8, 128) for k in range(6)]
    n_all = exact_dot(recv2[pl.ds(6, 32, stride=8), :], to_n_lanes)
    n = [F32(LEAF)] + [n_all[:, 128 * k : 128 * k + 128].reshape(4, 8, 128) for k in range(5)]
    rho = exact_dot(low_all, own) + exact_dot(jnp.broadcast_to(own[0:1], (8, 128)), top_all)[0:1]
    rho = rho.reshape(4, 8, 128)
    slot8 = lane8 >> 3

    def inner(s):
        y = s
        u = jnp.zeros_like(s)
        for h in range(5):
            y = y + xor_rows(y, 1 << h)
            u = u + w_low[h].reshape(4, 8, 128) * y
        t = y[0]
        top = jnp.zeros((8, 128), F32)
        for h in range(4):
            t = t + xor_lanes(t, slot8, 1 << h)
            top = top + w_top[h] * t
        return u + top[None]

    parts = [rho]
    sums = []
    for j in range(3):
        s = m[j]
        for k in range(j + 1):
            s = s + n[k] * parts[j - k]
        sums.append(s)
        parts.append(inner(s))
        rows_buf[j] = parts[j].reshape(32, 128)
    rows_buf[3] = parts[3].reshape(32, 128)

    def spread_of(c, u):
        return [sum(c[j] * u[j - k] for j in range(k, len(c))) for k in range(len(c))]

    def form(c, e, shift):
        whole = 0.0
        each = 0.0
        for j in range(len(c)):
            for k in range(j, len(c)):
                twice = 1.0 if j == k else 2.0
                t = j + k + shift
                whole = whole + (twice * c[j] * c[k]) * p[t]
                cross = c[j] * e[k] if j == k else c[j] * e[k] + c[k] * e[j]
                each = each + 2.0 * cross * m[t] + (twice * e[j]) * e[k] * n[t]
        return whole, each

    one = jnp.ones((8, 128), F32)
    d_c = [one]
    r_c = [one]
    x_c = [0.0, 0.0, 0.0]
    whole, each = form(d_c, [rho], 0)
    norm = whole + total(each)
    for it in range(3):
        d_e = spread_of(d_c, parts)
        image = sum(d_c[j] * parts[j + 1] for j in range(it + 1))
        whole, each = form(d_c, d_e, 1)
        curvature = whole + total(each + image * sum(d_c[j] * sums[j] for j in range(it + 1)))
        alpha = norm / curvature
        for k in range(it + 1):
            x_c[k] = x_c[k] + alpha * d_c[k]
        r_c = [a - alpha * i for a, i in zip(r_c + [0.0], [0.0] + d_c)]
        if it == 2:
            break
        whole, each = form(d_c, d_e, 2)
        along = sum(d_c[j] * m[j + 1] + d_e[j] * n[j + 1] for j in range(it + 1))
        square = whole + total(each + image * (2.0 * along + LEAF * image))
        after = alpha * alpha * square - norm
        beta = after / norm
        d_c = [a + beta * i for a, i in zip(r_c, d_c + [0.0])]
        norm = after

    mine = [rows_buf[k, pl.ds(b, 1), :] for k in range(4)]
    r_c = [c[0:1] for c in r_c]
    x_c = [c[0:1] for c in x_c]
    r_e = spread_of(r_c, mine)
    x_e = spread_of(x_c, mine)
    spare = jnp.zeros((1, 128), F32)
    values = r_e + x_e + [spare] + r_c[1:] + x_c + [spare, spare]
    back = jnp.concatenate([values[(16 - k) % 16] for k in range(16)], axis=0)
    send3[...] = turn_out(back).reshape(16, 1, 128)

    for offset in far_first((8, 2)):
        to = peer(g, offset, (8, 2))
        pltpu.make_async_remote_copy(
            src_ref=send3.at[lax.rem(16 - to, 16)], dst_ref=recv3.at[g], send_sem=ss3, recv_sem=rs3,
            device_id=(to, b), device_id_type=MESH,
        ).start()
    recv3[pl.ds(g, 1)] = send3[pl.ds(lax.rem(16 - g, 16), 1)]
    lift_r = jnp.zeros((128, 128), F32)
    lift_x = jnp.zeros((128, 128), F32)
    for k in range(4):
        lift_r = jnp.where(leaf_i == k, powers[k], lift_r)
        if k < 3:
            lift_x = jnp.where(leaf_i == 4 + k, powers[k], lift_x)
    lift = jnp.concatenate([lift_r.T[:, :16], lift_x.T[:, :16]], axis=0)
    pltpu.make_async_copy(recv3.at[pl.ds(0, GRP - 1)], recv3.at[pl.ds(0, GRP - 1)], rs3).wait()
    gains = turn_in(recv3[...].reshape(16, 128), g)
    gains = jnp.where((iota((16, 128), 1) & 7) == 7, 0.0, gains)
    lifted = exact_dot(lift, gains)
    r = lifted[:128] + v_buf[0]
    x = lifted[128:]
    for k in range(3):
        r = r + gains[8 + k : 9 + k] * v_buf[k + 1]
        x = x + gains[11 + k : 12 + k] * v_buf[k]
    x = x.T
    r = r.T
    for k in range(16):
        x_out[7 * k : 7 * k + 7, :] = x[8 * k : 8 * k + 7]
        r_out[7 * k : 7 * k + 7, :] = r[8 * k : 8 * k + 7]

    pltpu.make_async_copy(recv1.at[pl.ds(0, GRP - 1)], recv1.at[pl.ds(0, GRP - 1)], ss1).wait()
    pltpu.make_async_copy(recv2.at[pl.ds(0, 8 * (BASIN - 1))], recv2.at[pl.ds(0, 8 * (BASIN - 1))], ss2).wait()
    pltpu.make_async_copy(recv3.at[pl.ds(0, GRP - 1)], recv3.at[pl.ds(0, GRP - 1)], ss3).wait()


def hand_out(x, r, x_out, r_out, x_sem, r_sem):
    copies = [pltpu.make_async_copy(x, x_out, x_sem), pltpu.make_async_copy(r, r_out, r_sem)]
    for copy in copies:
        copy.start()
    for copy in copies:
        copy.wait()


def on_device(leaf_features, node_features, w_in, w_out, leaf_var, node_var, inner_var, sub_sizes):
    vmem = pl.BlockSpec(memory_space=pltpu.VMEM)
    hbm = pl.BlockSpec(memory_space=pltpu.HBM)
    tile = jax.ShapeDtypeStruct((112, 128), F32)
    x, r = pl.pallas_call(
        kernel,
        out_shape=(tile, tile),
        in_specs=[hbm] * 8,
        out_specs=(vmem, vmem),
        scratch_shapes=[
            pltpu.VMEM((16, 128, 128), BF16),
            pltpu.VMEM((11, 16, 128), BF16),
            pltpu.VMEM((512, 128), BF16),
            pltpu.VMEM((7, 512), BF16),
            pltpu.VMEM((1, 128), F32),
            pltpu.SMEM((1, 10), F32),
            pltpu.VMEM((1, 511), F32),
            pltpu.SMEM((1, 9), jnp.int32),
            pltpu.VMEM((4, 128, 128), F32),
            pltpu.VMEM((5, 32, 128), F32),
            pltpu.VMEM((4, 8, 128), F32),
            pltpu.VMEM((16, 1, 128), F32),
            pltpu.VMEM((16, 1, 128), F32),
            pltpu.VMEM((8, 128), F32),
            pltpu.VMEM((256, 128), F32),
            pltpu.VMEM((16, 1, 128), F32),
            pltpu.VMEM((16, 1, 128), F32),
            pltpu.VMEM((4, 32, 128), F32),
            pltpu.SemaphoreType.DMA((CHUNKS,)),
            pltpu.SemaphoreType.DMA((7,)),
        ]
        + [pltpu.SemaphoreType.DMA] * 6,
        compiler_params=pltpu.CompilerParams(collective_id=0, has_side_effects=True, vmem_limit_bytes=32 * 1024 * 1024),
    )(*[
        pltpu.with_memory_space_constraint(a, pltpu.HBM)
        for a in (
            leaf_features, jnp.transpose(node_features, (2, 0, 1)), w_in, w_out,
            leaf_var.reshape(1, -1), node_var.reshape(1, -1), inner_var.reshape(1, -1), sub_sizes,
        )
    ])

    here = pl.BlockSpec(memory_space=pl.ANY)
    return pl.pallas_call(
        hand_out,
        out_shape=(tile, tile),
        in_specs=[here] * 2,
        out_specs=(here, here),
        scratch_shapes=[pltpu.SemaphoreType.DMA, pltpu.SemaphoreType.DMA],
        compiler_params=pltpu.CompilerParams(vmem_limit_bytes=32 * 1024 * 1024),
    )(x, r)


def solution(mesh):
    return jax.shard_map(
        on_device,
        mesh=mesh,
        in_specs=(
            P(None, None, ("grp", "basin")),
            P(None, None, ("grp", "basin")),
            P(),
            P(),
            P(("grp", "basin")),
            P(("grp", "basin")),
            P(),
            P(("grp", "basin"), None),
        ),
        out_specs=(P(None, ("grp", "basin")), P(None, ("grp", "basin"))),
        check_vma=False,
    )
```
